512 devices in a mesh: grp: 2 (over core), reg: 16 (over z, x_hi), tgt: 16 (over y, x_lo).
Axes of the slice: x: 4 (x_hi: 2, x_lo: 2; x = x_hi * 2 + x_lo), y: 8, z: 8, core: 2. Of those that a mesh axis runs over, the one named last changes fastest.
Arguments:
- expr_stretch: bfloat16 [6144, 4096], P('reg'), may hold values from -6 to 6
- target_stretch: bfloat16 [6144, 1024], P('reg', 'tgt'), may hold values from -6 to 6
- subsample: int32 [2, 6144], replicated, may hold values 0 or 1
- gram_state: float32 [2, 2, 4096, 4096], P(None, 'grp', 'reg', 'tgt')
- cross_state: float32 [2, 2, 4096, 1024], P(None, 'grp', 'reg', 'tgt'), may hold values from -10 to 10
- step_size: float32 [2], replicated, may hold values from 0.15 to 0.25
- penalty: float32 [2], replicated, may hold values from 0.3 to 1
Outputs:
- gram_sums: float32 [2, 4096, 4096], P('grp', 'reg', 'tgt')
- cross_sums: float32 [2, 4096, 1024], P('grp', 'reg', 'tgt')
- coefficients: float32 [2, 4096, 1024], P('grp', 'reg', 'tgt')
The draws below stay inside these ranges and needn't reach their ends.
All inputs are finite; a program needn't handle non-finite values.
Results may differ from the reference program's by a relative error of at most 0.0021.
Values may be sent and summed in bfloat16 or wider, within the bound.
A program may use at most 64 MiB of HBM per device.

```python
import math
import jax
import jax.numpy as jnp
from jax import lax

REGS = 4096
ITERS = 3
CELLS = 6144
TARGETS = 1024


def draw_gram_state(key, part):
    key = jax.random.fold_in(key, 11)
    key_off, key_diag = jax.random.split(key)
    spread = 0.5 / math.sqrt(REGS)
    off_part = jax.random.normal(key_off, (2, 2, REGS, REGS), jnp.float32) * spread
    diag_part = jax.random.uniform(key_diag, (2, 2, REGS), jnp.float32, 2.0, 3.0)
    index_line = lax.iota(jnp.int32, REGS)
    same_spot = index_line[:, None] == index_line[None, :]
    return jnp.where(same_spot, diag_part[:, :, :, None], off_part)


def plant(drawn, own_key, least, high):
    spot = [jax.random.randint(jax.random.fold_in(own_key, axis), (), 0, length) for axis, length in enumerate(drawn.shape)]
    main_axis = drawn.shape.index(max(drawn.shape))
    next_to = spot[:main_axis] + [(spot[main_axis] + 1) % drawn.shape[main_axis]] + spot[main_axis + 1:]
    return drawn.at[tuple(spot)].set(least).at[tuple(next_to)].set(high)


def shard_levels(stream_key, extent, cuts, least, top_value):
    def one(position, parts):
        draws = jax.random.uniform(jax.random.fold_in(jax.random.fold_in(stream_key, 6), position), (parts,), jnp.float32, least / len(cuts), top_value / len(cuts))
        return jnp.repeat(jnp.exp(draws), extent[position] // parts).reshape((-1,) + (1,) * (len(extent) - position - 1))

    level = one(*cuts[0])
    for cut in cuts[1:]:
        level = level * one(*cut)
    return level


def bell_draw(key, dims, scale, most, shards=(), dtype=jnp.bfloat16):
    result = scale * jax.random.normal(key, dims, jnp.float32)
    if shards:
        result = result * shard_levels(key, dims, shards, -0.22, 0.18)
    return jnp.clip(result, -most, most).astype(dtype)


def setup_inputs(seed: int = 0) -> dict:
    arg_keys = jax.random.split(jax.random.key(seed), 8)
    return {
        "expr_stretch": bell_draw(arg_keys[0], (CELLS, REGS), 1.0, 6.0, ((0, 16),)),
        "target_stretch": bell_draw(arg_keys[1], (CELLS, TARGETS), 1.0, 6.0, ((0, 16), (1, 16))),
        "subsample": plant((jax.random.randint(arg_keys[2], (2, CELLS), 0, 2) < 1).astype(jnp.int32), jax.random.fold_in(arg_keys[2], 1), 0, 1),
        "gram_state": draw_gram_state(jax.random.fold_in(arg_keys[7], 71), 0),
        "cross_state": bell_draw(arg_keys[4], (2, 2, REGS, TARGETS), 2.0, 10.0, ((1, 2), (2, 16), (3, 16)), jnp.float32),
        "step_size": jnp.clip(jax.random.uniform(arg_keys[5], (2,), jnp.float32, 0.15, 0.25), 0.15, 0.25),
        "penalty": jnp.clip(jax.random.uniform(arg_keys[6], (2,), jnp.float32, 0.3, 1.0), 0.3, 1.0),
    }


def soften(values, threshold):
    return values - jnp.clip(values, -threshold, threshold)


def reference(expr_stretch, target_stretch, subsample, gram_state, cross_state, step_size, penalty):
    activity = expr_stretch.astype(jnp.float32)
    targets_f = target_stretch.astype(jnp.float32)
    weights_f = subsample.astype(jnp.float32)
    gram_terms = []
    cross_terms = []
    for replicate in range(2):
        weighted = activity * weights_f[replicate][:, None]
        gram_terms.append(jnp.dot(weighted.T, activity, preferred_element_type=jnp.float32, precision=lax.Precision.HIGHEST) / CELLS)
        cross_terms.append(jnp.dot(weighted.T, targets_f, preferred_element_type=jnp.float32, precision=lax.Precision.HIGHEST) / CELLS)
    gram_sums = gram_state[1] + jnp.stack(gram_terms)
    cross_sums = cross_state[1] + jnp.stack(cross_terms)
    gram_low = gram_state[0].astype(jnp.bfloat16).astype(jnp.float32)
    cross_now = cross_state[0]
    step_scale = step_size[:, None, None]
    threshold = step_scale * penalty[:, None, None]
    beta = soften(step_scale * cross_now, threshold)
    for iteration in range(ITERS - 1):
        beta_low = beta.astype(jnp.bfloat16).astype(jnp.float32)
        product = jnp.einsum("rik,rkj->rij", gram_low, beta_low, precision=lax.Precision.HIGHEST)
        beta = soften(beta - step_scale * (product - cross_now), threshold)
    return gram_sums, cross_sums, beta
```

```python
import jax
import jax.numpy as jnp
from jax import lax
from jax.experimental import pallas as pl
from jax.experimental.pallas import tpu as pltpu
from jax.sharding import PartitionSpec as P

RING = 8
CELLS = 6144
F32, BF16 = jnp.float32, jnp.bfloat16
ROWS_T = (((1,), (1,)), ((), ()))


def soften(values, threshold):
    return values - jnp.clip(values, -threshold, threshold)


def kernel(
    expr, target_hbm, subsample_hbm, gram_hbm, cross_hbm, step_hbm, penalty_hbm,
    gram_out, cross_out, coef_out,
    target, subsample, gram_state, cross_state, step_size, penalty,
    gbuf, bbuf, cross_fit, bsend, acc, precv,
    cbuf, rbuf, lhs, tpad, tsend, trecv, tgt_t, wbuf, gsend,
    xsend, xpass, own_block, xrecv, end_part, end_beta, beta_keep,
    ring_send, ring_recv, spread_send, spread_recv, piece_send, piece_recv,
    part_send, part_recv, far_send, far_recv, near_send, near_recv,
    feed_send, feed_recv, end_send, end_recv, own_send, own_recv,
    swap_send, swap_recv, local_sem, load_sem,
):
    c = lax.axis_index("grp")
    reg = lax.axis_index("reg")
    tgt = lax.axis_index("tgt")
    z, xh = reg // 2, reg % 2
    y, xl = tgt // 2, tgt % 2
    x = xh * 2 + xl

    def device(core, zz=z, hi=xh, yy=y, lo=xl):
        return (core, zz * 2 + hi, yy * 2 + lo)

    def chip_x(index, core):
        return device(core, hi=index // 2, lo=index % 2)

    def remote(src, dst, send, recv, to):
        return pltpu.make_async_remote_copy(
            src_ref=src, dst_ref=dst, send_sem=send, recv_sem=recv,
            device_id=to, device_id_type=pl.DeviceIdType.MESH,
        )

    right, left = (x + 1) % 4, (x + 3) % 4
    barrier = pltpu.get_barrier_semaphore()

    def greet(peers):
        for peer in peers:
            pl.semaphore_signal(barrier, inc=1, device_id=peer, device_id_type=pl.DeviceIdType.MESH)

    def load(index, source, here):
        copy = pltpu.make_async_copy(source, here, load_sem.at[index])
        copy.start()
        return copy

    def rings(core, view_of, along_y, sent):
        def ring_copy(ring, part, way, hop, chunk):
            here = y if ring in along_y else z
            there = (here + (1 if way == 0 else RING - 1)) % RING
            view = view_of(ring, part, chunk)
            slot = ring * 2 + part
            return remote(view, view, ring_send.at[slot, way, hop - 1], ring_recv.at[slot, way, hop - 1],
                          device(core, yy=there) if ring in along_y else device(core, zz=there))

        def ring_start(ring, part):
            here = y if ring in along_y else z
            for way in range(2):
                copy = ring_copy(ring, part, way, 1, here)
                copy.start()
                sent.append(copy)

        def ring_step(ring, part, hop):
            here = y if ring in along_y else z
            for way in range(2):
                if hop == 4 and way != part:
                    continue
                chunk = (here + (RING - hop if way == 0 else hop)) % RING
                ring_copy(ring, part, way, hop, chunk).wait_recv()
                if hop < 3 or (hop == 3 and way == part):
                    copy = ring_copy(ring, part, way, hop + 1, chunk)
                    copy.start()
                    sent.append(copy)

        return ring_start, ring_step

    @pl.when(c == 1)
    def _():
        GRAM, BETA = 0, 1
        loads = [
            load(0, step_hbm, step_size), load(1, penalty_hbm, penalty),
            load(2, cross_hbm, cross_state), load(3, gram_hbm, gram_state),
        ]
        peers = [device(1, zz=(z + d) % RING) for d in (1, 7)]
        peers += [device(1, yy=(y + d) % RING) for d in (1, 7)]
        peers += [chip_x((x + d) % 4, 1) for d in (1, 2, 3)]
        peers += [chip_x(right, 0), chip_x(left, 0), device(0)]
        greet(peers)
        sent = []

        def start(copy):
            copy.start()
            sent.append(copy)

        def view_of(ring, part, chunk):
            if ring == GRAM:
                return gbuf.at[part, chunk]
            return bbuf.at[ring - BETA, part, chunk]

        ring_start, ring_step = rings(1, view_of, (GRAM,), sent)
        own_k = xl == xh

        def own_half(ref_index):
            return pl.ds(pl.multiple_of(ref_index * 64, 64), 64)

        def piece_slot(it, r, lo):
            return bbuf.at[it, r, z, own_half(lo)]

        def piece_near(it, r):
            return remote(bsend.at[it, r], piece_slot(it, r, xl), piece_send.at[it, r, 1],
                          piece_recv.at[it, r, xl], device(1, lo=1 - xl))

        def pieces_start(it, r):
            start(remote(bsend.at[it, r], piece_slot(it, r, xl), piece_send.at[it, r, 0],
                         piece_recv.at[it, r, xl], device(1, hi=1 - xh, lo=xh)))

            @pl.when(own_k)
            def _():
                pltpu.make_async_copy(
                    bsend.at[it, r], piece_slot(it, r, xl), piece_recv.at[it, r, xl]).start()

            @pl.when(jnp.logical_not(own_k))
            def _():
                piece_near(it, r).start()

        def pieces_wait(it, r):
            for lo in range(2):
                pltpu.make_async_copy(
                    bsend.at[it, r], piece_slot(it, r, lo), piece_recv.at[it, r, lo]).wait()

        def add_products(it, r, distances, first=False):
            total = None
            for distance in distances:
                k = (y + distance) % RING if it == 0 else (z + distance) % RING
                term = lax.dot_general(bbuf[it, r, k], gbuf[r, k], ROWS_T, preferred_element_type=F32)
                total = term if total is None else total + term
            acc[it, r] = total if first else acc[it, r] + total

        def part_copy(it, r):
            return remote(acc.at[it, r, own_half(1 - xl)], precv.at[it, r],
                          part_send.at[it, r], part_recv.at[it, r], device(1, lo=1 - xl))

        def step_of(r):
            return step_size[r], step_size[r] * penalty[r]

        def next_beta(it, r, beta):
            step, threshold = step_of(r)
            part_copy(it, r).wait_recv()
            product = acc[it, r, own_half(xl)] + precv[it, r]
            return soften(beta - step * (product - cross_fit[r]), threshold)

        for copy in loads:
            copy.wait()
        gbuf[1, y] = gram_state[0].astype(BF16)
        cross_fit[1] = cross_state[0]
        step, threshold = step_of(1)
        beta_one = soften(step * cross_state[0], threshold)
        bsend[0, 1] = beta_one.astype(BF16)
        pl.semaphore_wait(barrier, len(peers))

        ring_start(GRAM, 1)
        pieces_start(0, 1)
        cross_feed = remote(cross_state.at[0], cross_fit.at[0], feed_send.at[1], feed_recv.at[1], device(0))
        gram_feed = remote(gsend, gbuf.at[0, y], feed_send.at[0], feed_recv.at[0], device(0))
        gram_feed.wait_recv()
        ring_start(GRAM, 0)
        cross_feed.wait_recv()
        step, threshold = step_of(0)
        beta_zero = soften(step * cross_fit[0], threshold)
        bsend[0, 0] = beta_zero.astype(BF16)
        pieces_start(0, 0)
        for r in (1, 0):
            pieces_wait(0, r)
            ring_start(BETA, r)
        for hop in (1, 2, 3):
            for r in (1, 0):
                ring_step(GRAM, r, hop)
            for r in (1, 0):
                ring_step(BETA, r, hop)
        for r in (1, 0):
            ring_step(GRAM, r, 4)
            ring_step(BETA, r, 4)
            add_products(0, r, range(RING), first=True)
            start(part_copy(0, r))
        betas = [beta_zero, beta_one]
        for r in (1, 0):
            betas[r] = next_beta(0, r, betas[r])
            bsend[1, r] = betas[r].astype(BF16)
            pieces_start(1, r)
        beta_keep[...] = betas[0]
        start(remote(beta_keep, end_beta, end_send.at[2], end_recv.at[2], device(0)))
        for r in (1, 0):
            pieces_wait(1, r)
            ring_start(BETA + 1, r)
        for hop in (1, 2, 3):
            for r in (1, 0):
                ring_step(BETA + 1, r, hop)
            for r in (1, 0):
                if hop == 1:
                    add_products(1, r, (0,), first=True)
                else:
                    add_products(1, r, (hop - 1, RING + 1 - hop))
        ring_step(BETA + 1, 1, 4)
        add_products(1, 1, (3, 5, 4))
        start(part_copy(1, 1))
        ring_step(BETA + 1, 0, 4)
        add_products(1, 0, (3, 5, 4))
        start(remote(acc.at[1, 0, own_half(1 - xl)], end_part.at[1], end_send.at[1], end_recv.at[1],
                     device(0, lo=1 - xl)))
        start(remote(acc.at[1, 0, own_half(xl)], end_part.at[0], end_send.at[0], end_recv.at[0], device(0)))
        coef_out[...] = next_beta(1, 1, betas[1])

        for copy in sent:
            copy.wait_send()
        for it in range(2):
            for r in range(2):
                @pl.when(jnp.logical_not(own_k))
                def _():
                    piece_near(it, r).wait_send()

    @pl.when(c == 0)
    def _():
        COLS, ROWS = 0, 1
        row0 = pl.multiple_of(xl * 192, 16)
        row0_other = pl.multiple_of((1 - xl) * 192, 16)
        part_h, part_q = y // 4, y % 4
        rows_h = pl.multiple_of(xl * 192 + part_h * 96, 16)

        def at96(index):
            return pl.ds(pl.multiple_of(index * 96, 16), 96)

        def expr_cols(index):
            return pl.ds(pl.multiple_of(index * 512 + part_q * 128, 128), 128)

        loads = [
            load(3, gram_hbm, gram_state), load(2, cross_hbm, cross_state), load(4, target_hbm, target),
            load(0, step_hbm, step_size), load(1, penalty_hbm, penalty), load(5, subsample_hbm, subsample),
        ]
        peers = [device(0, zz=(z + d) % RING) for d in range(1, RING)]
        peers += [device(0, yy=(y + d) % RING) for d in (1, 7)]
        peers += [chip_x(right, 0), chip_x(left, 0), chip_x(right, 1), chip_x(left, 1), device(1)]
        greet(peers)
        local = [
            pltpu.make_async_copy(
                expr.at[pl.ds(pl.multiple_of(row0 + h * 96, 16), 96), pl.ds(pl.multiple_of(y * 512, 512), 512)],
                cbuf.at[h, z, :, pl.ds(0, 512)], local_sem.at[h])
            for h in range(2)
        ]
        local.append(pltpu.make_async_copy(
            expr.at[pl.ds(rows_h, 96), expr_cols(z)], rbuf.at[y, at96(z)], local_sem.at[2]))
        for copy in local:
            copy.start()
        sent = []

        def start(copy):
            copy.start()
            sent.append(copy)

        def view_of(ring, part, chunk):
            if ring == COLS:
                return cbuf.at[part, chunk]
            return rbuf.at[chunk, pl.ds(part * 384, 384)]

        ring_start, ring_step = rings(0, view_of, (ROWS,), sent)

        loads[0].wait()
        gsend[...] = gram_state[0].astype(BF16)
        loads[1].wait()
        loads[2].wait()
        both = jnp.concatenate([target[...], target[...]], axis=0)
        lane_half = lax.broadcasted_iota(jnp.int32, both.shape, 0) // 64
        both = jnp.where(lane_half == xl, both, jnp.zeros_like(both))
        tpad[...] = both.T
        tsend[...] = tpad[pl.ds(row0_other, 192), :]
        pl.semaphore_wait(barrier, len(peers))

        start(remote(gsend, gbuf.at[0, y], feed_send.at[0], feed_recv.at[0], device(1)))
        start(remote(cross_state.at[0], cross_fit.at[0], feed_send.at[1], feed_recv.at[1], device(1)))
        swap = remote(tsend, trecv, swap_send, swap_recv, device(0, lo=1 - xl))
        start(swap)
        for d in range(1, RING):
            to = (z + d) % RING
            start(remote(expr.at[pl.ds(rows_h, 96), expr_cols(to)], rbuf.at[y, at96(z)],
                         spread_send.at[d - 1], spread_recv.at[d - 1], device(0, zz=to)))
        swap.wait_recv()
        for h in range(2):
            cbuf[h, z, :, 512:640] = (
                tpad[pl.ds(pl.multiple_of(row0 + h * 96, 16), 96), :] + trecv[h * 96:(h + 1) * 96, :])
        for copy in local:
            copy.wait()
        for part in range(2):
            ring_start(COLS, part)
        for d in range(1, RING):
            source = (z + RING - d) % RING
            remote(expr.at[pl.ds(rows_h, 96), expr_cols(z)], rbuf.at[y, at96(source)],
                   spread_send.at[d - 1], spread_recv.at[d - 1], device(0, zz=source)).wait_recv()
        for part in range(2):
            ring_start(ROWS, part)

        for copy in loads[3:]:
            copy.wait()
        first_lane = xh * 384 + xl * 192
        lane = lax.broadcasted_iota(jnp.int32, (2, 768), 1)
        for h in range(2):
            weights = jnp.zeros((2, 768), F32)
            for zz in range(RING):
                cells = subsample[:, zz * 768:(zz + 1) * 768].astype(F32)
                moved = pltpu.roll(cells, (1536 + zz * 96 - h * 96 - first_lane) % 768, axis=1)
                weights = jnp.where((lane >= zz * 96) & (lane < zz * 96 + 96), moved, weights)
            wbuf[h] = weights

        def weigh(distance):
            chunk = (y + distance) % RING
            h, q = chunk // 4, chunk % 4
            block = rbuf[chunk].T
            rows = pl.ds(pl.multiple_of(q * 128, 128), 128)
            pair = wbuf[h].astype(BF16)
            for r in range(2):
                lhs[r, h, rows, :] = block * pair[r:r + 1, :]

        weigh(0)
        for hop in (1, 2, 3):
            for part in range(2):
                ring_step(ROWS, part, hop)
            for part in range(2):
                ring_step(COLS, part, hop)
            weigh(hop)
            weigh(RING - hop)
        for part in range(2):
            ring_step(COLS, part, 4)
        for h in range(2):
            tgt_t[h] = cbuf[h, :, :, 512:640].reshape(768, 128).T
        for part in range(2):
            ring_step(ROWS, part, 4)
        weigh(4)

        def sums_of(r, index):
            hi, lo = index // 2, index % 2
            gram = jnp.zeros((256, 256), F32)
            crosses = jnp.zeros((64, 256), F32)
            for h in range(2):
                rows = lhs[r, h, pl.ds(pl.multiple_of(hi * 256, 256), 256), :]
                cols = cbuf[h, :, :, pl.ds(pl.multiple_of(lo * 256, 256), 256)].reshape(768, 256)
                gram += jnp.dot(rows, cols, preferred_element_type=F32)
                crosses += lax.dot_general(
                    tgt_t[h, pl.ds(pl.multiple_of(lo * 64, 64), 64), :], rows, ROWS_T, preferred_element_type=F32)
            return gram, crosses

        top, low = pl.ds(0, 160), pl.ds(160, 160)

        def far_copy(r, half):
            rows = low if half else top
            return remote(xsend.at[r, 0, rows], xpass.at[r, rows], far_send.at[r, half], far_recv.at[r, half],
                          chip_x(left if half else right, 0))

        def near_copy(r, way, half):
            rows = low if half else top
            return remote(xsend.at[r, 1 + way, rows], xrecv.at[way, rows], near_send.at[r, way, half],
                          near_recv.at[way, half], chip_x(left if way else right, r))

        for r in (1, 0):
            gram, crosses = sums_of(r, (x + 2) % 4)
            xsend[r, 0, 0:256, :] = gram.astype(BF16)
            xsend[r, 0, 256:320, :] = crosses.astype(BF16)
            start(far_copy(r, 0))
            start(far_copy(r, 1))
        for r in (1, 0):
            gram, crosses = sums_of(r, right)
            xsend[r, 1, 160:256, :] = gram[160:256].astype(BF16)
            xsend[r, 1, 256:320, :] = crosses.astype(BF16)
            start(near_copy(r, 0, 1))
            far_copy(r, 0).wait_recv()
            xsend[r, 1, 0:160, :] = (gram[0:160] + xpass[r, 0:160, :].astype(F32)).astype(BF16)
            start(near_copy(r, 0, 0))
            gram, crosses = sums_of(r, left)
            xsend[r, 2, 0:160, :] = gram[0:160].astype(BF16)
            start(near_copy(r, 1, 0))
            far_copy(r, 1).wait_recv()
            xsend[r, 2, 160:256, :] = (gram[160:256] + xpass[r, 160:256, :].astype(F32)).astype(BF16)
            xsend[r, 2, 256:320, :] = (crosses + xpass[r, 256:320, :].astype(F32)).astype(BF16)
            start(near_copy(r, 1, 1))
        gram, crosses = sums_of(1, x)
        xsend_own = own_block.at[1]
        own_block[1, 0:256, :] = gram
        own_block[1, 256:320, :] = crosses
        start(remote(xsend_own, own_block.at[0], own_send, own_recv, device(1)))
        gram, crosses = sums_of(0, x)
        own_block[0, 0:256, :] = gram
        own_block[0, 256:320, :] = crosses

        for i in range(3):
            remote(end_beta, end_beta if i == 2 else end_part.at[i], end_send.at[i], end_recv.at[i],
                   device(1)).wait_recv()
        step = step_size[0]
        product = end_part[0] + end_part[1]
        coef_out[...] = soften(end_beta[...] - step * (product - cross_state[0]), step * penalty[0])
        for copy in sent:
            copy.wait_send()

    @pl.when(c == 1)
    def _():
        remote(own_block.at[1], own_block.at[0], own_send, own_recv, device(0)).wait_recv()

    for way in range(2):
        for half in range(2):
            rows = pl.ds(160 * half, 160)
            remote(xsend.at[0, 1 + way, rows], xrecv.at[way, rows], near_send.at[0, way, half],
                   near_recv.at[way, half], chip_x(left if way else right, 0)).wait_recv()
    sums = own_block[0] + xrecv[0].astype(F32) + xrecv[1].astype(F32)
    gram_out[...] = gram_state[1] + sums[0:256] / CELLS
    cross_out[...] = cross_state[1] + sums[256:320] / CELLS


def copy_out(gram, cross, coef, gram_out, cross_out, coef_out, gram_here, cross_here, coef_here, sems_in, sems_out):
    stages = ((gram, gram_here, gram_out), (cross, cross_here, cross_out), (coef, coef_here, coef_out))
    ins = [pltpu.make_async_copy(source, here, sems_in.at[i]) for i, (source, here, _) in enumerate(stages)]
    outs = [pltpu.make_async_copy(here, out, sems_out.at[i]) for i, (_, here, out) in enumerate(stages)]
    for copy in ins:
        copy.start()
    for arrived, copy in zip(ins, outs):
        arrived.wait()
        copy.start()
    for copy in outs:
        copy.wait()


def body(expr_stretch, target_stretch, subsample, gram_state, cross_state, step_size, penalty):
    vmem = pl.BlockSpec(memory_space=pltpu.VMEM)
    hbm = pl.BlockSpec(memory_space=pltpu.HBM)
    dma = pltpu.SemaphoreType.DMA
    out_shape = (
        jax.ShapeDtypeStruct((256, 256), F32),
        jax.ShapeDtypeStruct((64, 256), F32),
        jax.ShapeDtypeStruct((64, 256), F32),
    )
    results = pl.pallas_call(
        kernel,
        out_shape=out_shape,
        in_specs=[hbm] * 7,
        out_specs=(vmem, vmem, vmem),
        scratch_shapes=[
            pltpu.VMEM((64, 384), BF16),
            pltpu.VMEM((2, CELLS), jnp.int32),
            pltpu.VMEM((2, 256, 256), F32),
            pltpu.VMEM((2, 64, 256), F32),
            pltpu.SMEM((2,), F32),
            pltpu.SMEM((2,), F32),
            pltpu.VMEM((2, RING, 256, 256), BF16),
            pltpu.VMEM((2, 2, RING, 128, 256), BF16),
            pltpu.VMEM((2, 64, 256), F32),
            pltpu.VMEM((2, 2, 64, 256), BF16),
            pltpu.VMEM((2, 2, 128, 256), F32),
            pltpu.VMEM((2, 2, 64, 256), F32),
            pltpu.VMEM((2, RING, 96, 640), BF16),
            pltpu.VMEM((RING, 768, 128), BF16),
            pltpu.VMEM((2, 2, 512, 768), BF16),
            pltpu.VMEM((384, 128), BF16),
            pltpu.VMEM((192, 128), BF16),
            pltpu.VMEM((192, 128), BF16),
            pltpu.VMEM((2, 128, 768), BF16),
            pltpu.VMEM((2, 2, 768), F32),
            pltpu.VMEM((256, 256), BF16),
            pltpu.VMEM((2, 3, 320, 256), BF16),
            pltpu.VMEM((2, 320, 256), BF16),
            pltpu.VMEM((2, 320, 256), F32),
            pltpu.VMEM((2, 320, 256), BF16),
            pltpu.VMEM((2, 64, 256), F32),
            pltpu.VMEM((64, 256), F32),
            pltpu.VMEM((64, 256), F32),
            dma((6, 2, 4)), dma((6, 2, 4)),
            dma((7,)), dma((7,)),
            dma((2, 2, 2)), dma((2, 2, 2)),
            dma((2, 2)), dma((2, 2)),
            dma((2, 2)), dma((2, 2)),
            dma((2, 2, 2)), dma((2, 2)),
            dma((2,)), dma((2,)),
            dma((3,)), dma((3,)),
            dma, dma,
            dma, dma,
            dma((3,)),
            dma((6,)),
        ],
        compiler_params=pltpu.CompilerParams(
            collective_id=0, has_side_effects=True, vmem_limit_bytes=60 * 2**20),
    )(
        expr_stretch,
        target_stretch.T,
        subsample,
        gram_state[:, 0],
        jnp.swapaxes(cross_state[:, 0], 1, 2),
        step_size,
        penalty,
    )
    gram, cross, coef = pl.pallas_call(
        copy_out,
        out_shape=out_shape,
        in_specs=[hbm] * 3,
        out_specs=(hbm, hbm, hbm),
        scratch_shapes=[
            pltpu.VMEM((256, 256), F32),
            pltpu.VMEM((64, 256), F32),
            pltpu.VMEM((64, 256), F32),
            dma((3,)),
            dma((3,)),
        ],
        compiler_params=pltpu.CompilerParams(vmem_limit_bytes=60 * 2**20),
    )(*results)
    return gram[None], cross.T[None], coef.T[None]


def solution(mesh):
    return jax.shard_map(
        body,
        mesh=mesh,
        in_specs=(
            P("reg", None),
            P("reg", "tgt"),
            P(),
            P(None, "grp", "reg", "tgt"),
            P(None, "grp", "reg", "tgt"),
            P(),
            P(),
        ),
        out_specs=(P("grp", "reg", "tgt"), P("grp", "reg", "tgt"), P("grp", "reg", "tgt")),
        check_vma=False,
    )
```

```python
import jax
import jax.numpy as jnp
from jax import lax
from jax.experimental import pallas as pl
from jax.experimental.pallas import tpu as pltpu
from jax.sharding import PartitionSpec as P

RING = 8
CELLS = 6144
F32, BF16 = jnp.float32, jnp.bfloat16
ROWS_T = (((1,), (1,)), ((), ()))


def soften(values, threshold):
    return values - jnp.clip(values, -threshold, threshold)


def kernel(
    expr, target_hbm, subsample_hbm, gram_hbm, cross_hbm, step_hbm, penalty_hbm,
    gram_out, cross_out, coef_out,
    target, subsample, gram_state, cross_state, step_size, penalty,
    gbuf, bbuf, cross_fit, bsend, acc, precv,
    cbuf, tbuf, rbuf, lhs, tpad, tsend, trecv, crosses, wbuf, gsend,
    xsend, xpass, own_block, xrecv, end_part, end_beta, beta_keep,
    ring_send, ring_recv, spread_send, spread_recv, piece_send, piece_recv,
    part_send, part_recv, far_send, far_recv, near_send, near_recv,
    feed_send, feed_recv, end_send, end_recv, own_send, own_recv,
    swap_send, swap_recv, local_sem, load_sem,
):
    c = lax.axis_index("grp")
    reg = lax.axis_index("reg")
    tgt = lax.axis_index("tgt")
    z, xh = reg // 2, reg % 2
    y, xl = tgt // 2, tgt % 2
    x = xh * 2 + xl

    def device(core, zz=z, hi=xh, yy=y, lo=xl):
        return (core, zz * 2 + hi, yy * 2 + lo)

    def chip_x(index, core):
        return device(core, hi=index // 2, lo=index % 2)

    def remote(src, dst, send, recv, to):
        return pltpu.make_async_remote_copy(
            src_ref=src, dst_ref=dst, send_sem=send, recv_sem=recv,
            device_id=to, device_id_type=pl.DeviceIdType.MESH,
        )

    right, left = (x + 1) % 4, (x + 3) % 4
    barrier = pltpu.get_barrier_semaphore()

    def greet(peers):
        for peer in peers:
            pl.semaphore_signal(barrier, inc=1, device_id=peer, device_id_type=pl.DeviceIdType.MESH)

    def load(index, source, here):
        copy = pltpu.make_async_copy(source, here, load_sem.at[index])
        copy.start()
        return copy

    def rings(core, view_of, along_y, sent):
        def ring_copy(ring, part, way, hop, chunk):
            here = y if ring in along_y else z
            there = (here + (1 if way == 0 else RING - 1)) % RING
            view = view_of(ring, part, chunk)
            slot = ring * 2 + part
            return remote(view, view, ring_send.at[slot, way, hop - 1], ring_recv.at[slot, way, hop - 1],
                          device(core, yy=there) if ring in along_y else device(core, zz=there))

        def ring_start(ring, part):
            here = y if ring in along_y else z
            for way in range(2):
                copy = ring_copy(ring, part, way, 1, here)
                copy.start()
                sent.append(copy)

        def ring_step(ring, part, hop):
            here = y if ring in along_y else z
            for way in range(2):
                if hop == 4 and way != part:
                    continue
                chunk = (here + (RING - hop if way == 0 else hop)) % RING
                ring_copy(ring, part, way, hop, chunk).wait_recv()
                if hop < 3 or (hop == 3 and way == part):
                    copy = ring_copy(ring, part, way, hop + 1, chunk)
                    copy.start()
                    sent.append(copy)

        return ring_start, ring_step

    @pl.when(c == 1)
    def _():
        GRAM, BETA = 0, 1
        loads = [
            load(0, step_hbm, step_size), load(1, penalty_hbm, penalty),
            load(2, cross_hbm, cross_state), load(3, gram_hbm, gram_state),
        ]
        peers = [device(1, zz=(z + d) % RING) for d in (1, 7)]
        peers += [device(1, yy=(y + d) % RING) for d in (1, 7)]
        peers += [chip_x((x + d) % 4, 1) for d in (1, 2, 3)]
        peers += [chip_x(right, 0), chip_x(left, 0), device(0)]
        greet(peers)
        sent = []

        def start(copy):
            copy.start()
            sent.append(copy)

        def view_of(ring, part, chunk):
            if ring == GRAM:
                return gbuf.at[part, chunk]
            return bbuf.at[ring - BETA, part, chunk]

        ring_start, ring_step = rings(1, view_of, (GRAM,), sent)
        own_k = xl == xh

        def own_half(ref_index):
            return pl.ds(pl.multiple_of(ref_index * 64, 64), 64)

        def piece_slot(it, r, lo):
            return bbuf.at[it, r, z, own_half(lo)]

        def piece_near(it, r):
            return remote(bsend.at[it, r], piece_slot(it, r, xl), piece_send.at[it, r, 1],
                          piece_recv.at[it, r, xl], device(1, lo=1 - xl))

        def pieces_start(it, r):
            start(remote(bsend.at[it, r], piece_slot(it, r, xl), piece_send.at[it, r, 0],
                         piece_recv.at[it, r, xl], device(1, hi=1 - xh, lo=xh)))

            @pl.when(own_k)
            def _():
                pltpu.make_async_copy(
                    bsend.at[it, r], piece_slot(it, r, xl), piece_recv.at[it, r, xl]).start()

            @pl.when(jnp.logical_not(own_k))
            def _():
                piece_near(it, r).start()

        def pieces_wait(it, r):
            for lo in range(2):
                pltpu.make_async_copy(
                    bsend.at[it, r], piece_slot(it, r, lo), piece_recv.at[it, r, lo]).wait()

        def add_products(it, r, distances, first=False):
            total = None
            for distance in distances:
                k = (y + distance) % RING if it == 0 else (z + distance) % RING
                term = lax.dot_general(bbuf[it, r, k], gbuf[r, k], ROWS_T, preferred_element_type=F32)
                total = term if total is None else total + term
            acc[it, r] = total if first else acc[it, r] + total

        def part_copy(it, r):
            return remote(acc.at[it, r, own_half(1 - xl)], precv.at[it, r],
                          part_send.at[it, r], part_recv.at[it, r], device(1, lo=1 - xl))

        def step_of(r):
            return step_size[r], step_size[r] * penalty[r]

        def next_beta(it, r, beta):
            step, threshold = step_of(r)
            part_copy(it, r).wait_recv()
            product = acc[it, r, own_half(xl)] + precv[it, r]
            return soften(beta - step * (product - cross_fit[r]), threshold)

        for copy in loads:
            copy.wait()
        gbuf[1, y] = gram_state[0].astype(BF16)
        cross_fit[1] = cross_state[0]
        step, threshold = step_of(1)
        beta_one = soften(step * cross_state[0], threshold)
        bsend[0, 1] = beta_one.astype(BF16)
        pl.semaphore_wait(barrier, len(peers))

        ring_start(GRAM, 1)
        pieces_start(0, 1)
        cross_feed = remote(cross_state.at[0], cross_fit.at[0], feed_send.at[1], feed_recv.at[1], device(0))
        gram_feed = remote(gsend, gbuf.at[0, y], feed_send.at[0], feed_recv.at[0], device(0))
        gram_feed.wait_recv()
        ring_start(GRAM, 0)
        cross_feed.wait_recv()
        step, threshold = step_of(0)
        beta_zero = soften(step * cross_fit[0], threshold)
        bsend[0, 0] = beta_zero.astype(BF16)
        pieces_start(0, 0)
        for r in (1, 0):
            ring_step(GRAM, r, 1)
            pieces_wait(0, r)
            ring_start(BETA, r)
        for r in (1, 0):
            ring_step(BETA, r, 1)
        for r in (1, 0):
            ring_step(GRAM, r, 2)
        for r in (1, 0):
            ring_step(BETA, r, 2)
        for r in (1, 0):
            ring_step(GRAM, r, 3)
        for hop in (3, 4):
            for r in (1, 0):
                ring_step(BETA, r, hop)
        for r in (1, 0):
            add_products(0, r, (0, 1, 2, 3, 5, 6, 7), first=True)
        for r in (1, 0):
            ring_step(GRAM, r, 4)
            add_products(0, r, (4,))
            start(part_copy(0, r))
        betas = [beta_zero, beta_one]
        for r in (1, 0):
            betas[r] = next_beta(0, r, betas[r])
            bsend[1, r] = betas[r].astype(BF16)
            pieces_start(1, r)
        beta_keep[...] = betas[0]
        start(remote(beta_keep, end_beta, end_send.at[2], end_recv.at[2], device(0)))
        for r in (1, 0):
            pieces_wait(1, r)
            ring_start(BETA + 1, r)
        for hop in (1, 2, 3):
            for r in (1, 0):
                ring_step(BETA + 1, r, hop)
            for r in (1, 0):
                if hop == 1:
                    add_products(1, r, (0,), first=True)
                else:
                    add_products(1, r, (hop - 1, RING + 1 - hop))
        ring_step(BETA + 1, 1, 4)
        add_products(1, 1, (3, 5, 4))
        start(part_copy(1, 1))
        ring_step(BETA + 1, 0, 4)
        add_products(1, 0, (3, 5, 4))
        start(remote(acc.at[1, 0, own_half(1 - xl)], end_part.at[1], end_send.at[1], end_recv.at[1],
                     device(0, lo=1 - xl)))
        start(remote(acc.at[1, 0, own_half(xl)], end_part.at[0], end_send.at[0], end_recv.at[0], device(0)))
        coef_out[...] = next_beta(1, 1, betas[1])

        for copy in sent:
            copy.wait_send()
        for it in range(2):
            for r in range(2):
                @pl.when(jnp.logical_not(own_k))
                def _():
                    piece_near(it, r).wait_send()

    @pl.when(c == 0)
    def _():
        COLS, ROWS, TARGETS = 0, 1, 2
        row0 = pl.multiple_of(xl * 192, 16)
        row0_other = pl.multiple_of((1 - xl) * 192, 16)
        part_h, part_q = y // 4, y % 4
        rows_h = pl.multiple_of(xl * 192 + part_h * 96, 16)

        def at96(index):
            return pl.ds(pl.multiple_of(index * 96, 16), 96)

        def expr_cols(index):
            return pl.ds(pl.multiple_of(index * 512 + part_q * 128, 128), 128)

        loads = [
            load(3, gram_hbm, gram_state), load(2, cross_hbm, cross_state), load(4, target_hbm, target),
            load(0, step_hbm, step_size), load(1, penalty_hbm, penalty), load(5, subsample_hbm, subsample),
        ]
        peers = [device(0, zz=(z + d) % RING) for d in range(1, RING)]
        peers += [device(0, yy=(y + d) % RING) for d in (1, 7)]
        peers += [chip_x(right, 0), chip_x(left, 0), chip_x(right, 1), chip_x(left, 1), device(1)]
        greet(peers)
        local = [
            pltpu.make_async_copy(
                expr.at[pl.ds(pl.multiple_of(row0 + h * 96, 16), 96), pl.ds(pl.multiple_of(y * 512, 512), 512)],
                cbuf.at[h, z], local_sem.at[h])
            for h in range(2)
        ]
        local.append(pltpu.make_async_copy(
            expr.at[pl.ds(rows_h, 96), expr_cols(z)], rbuf.at[y, at96(z)], local_sem.at[2]))
        for copy in local:
            copy.start()
        sent = []

        def start(copy):
            copy.start()
            sent.append(copy)

        def view_of(ring, part, chunk):
            if ring == COLS:
                return cbuf.at[part, chunk]
            if ring == TARGETS:
                return tbuf.at[chunk]
            return rbuf.at[chunk, pl.ds(part * 384, 384)]

        ring_start, ring_step = rings(0, view_of, (ROWS,), sent)

        loads[0].wait()
        gsend[...] = gram_state[0].astype(BF16)
        loads[1].wait()
        loads[2].wait()
        both = jnp.concatenate([target[...], target[...]], axis=0)
        lane_half = lax.broadcasted_iota(jnp.int32, both.shape, 0) // 64
        both = jnp.where(lane_half == xl, both, jnp.zeros_like(both))
        tpad[...] = both.T
        tsend[...] = tpad[pl.ds(row0_other, 192), :]
        pl.semaphore_wait(barrier, len(peers))

        start(remote(gsend, gbuf.at[0, y], feed_send.at[0], feed_recv.at[0], device(1)))
        start(remote(cross_state.at[0], cross_fit.at[0], feed_send.at[1], feed_recv.at[1], device(1)))
        swap = remote(tsend, trecv, swap_send, swap_recv, device(0, lo=1 - xl))
        start(swap)
        for d in range(1, RING):
            to = (z + d) % RING
            start(remote(expr.at[pl.ds(rows_h, 96), expr_cols(to)], rbuf.at[y, at96(z)],
                         spread_send.at[d - 1], spread_recv.at[d - 1], device(0, zz=to)))
        for copy in local:
            copy.wait()
        for part in range(2):
            ring_start(COLS, part)
        swap.wait_recv()
        for h in range(2):
            tbuf[z, h] = (
                tpad[pl.ds(pl.multiple_of(row0 + h * 96, 16), 96), :] + trecv[h * 96:(h + 1) * 96, :])
        ring_start(TARGETS, 0)
        for d in range(1, RING):
            source = (z + RING - d) % RING
            remote(expr.at[pl.ds(rows_h, 96), expr_cols(z)], rbuf.at[y, at96(source)],
                   spread_send.at[d - 1], spread_recv.at[d - 1], device(0, zz=source)).wait_recv()
        for part in range(2):
            ring_start(ROWS, part)

        for copy in loads[3:]:
            copy.wait()
        first_lane = xh * 384 + xl * 192
        lane = lax.broadcasted_iota(jnp.int32, (2, 768), 1)
        for h in range(2):
            weights = jnp.zeros((2, 768), F32)
            for zz in range(RING):
                cells = subsample[:, zz * 768:(zz + 1) * 768].astype(F32)
                moved = pltpu.roll(cells, (1536 + zz * 96 - h * 96 - first_lane) % 768, axis=1)
                weights = jnp.where((lane >= zz * 96) & (lane < zz * 96 + 96), moved, weights)
            wbuf[h] = weights

        def weigh(distance):
            chunk = (y + distance) % RING
            h, q = chunk // 4, chunk % 4
            block = rbuf[chunk].T
            rows = pl.ds(pl.multiple_of(q * 128, 128), 128)
            pair = wbuf[h].astype(BF16)
            for r in range(2):
                lhs[r, h, rows, :] = block * pair[r:r + 1, :]

        weigh(0)
        for hop in (1, 2, 3):
            for part in range(2):
                ring_step(ROWS, part, hop)
            for part in range(2):
                ring_step(COLS, part, hop)
            ring_step(TARGETS, 0, hop)
            weigh(hop)
            weigh(RING - hop)
        for part in range(2):
            ring_step(COLS, part, 4)
        ring_step(TARGETS, 0, 4)
        for part in range(2):
            ring_step(ROWS, part, 4)
        weigh(4)

        def rows_of(hi, h):
            half = pl.ds(pl.multiple_of(hi * 256, 256), 256)
            return jnp.concatenate([lhs[0, h, half, :], lhs[1, h, half, :]], axis=0)

        def grams_of(index):
            hi, lo = index // 2, index % 2
            total = jnp.zeros((512, 256), F32)
            for h in range(2):
                cols = cbuf[h, :, :, pl.ds(pl.multiple_of(lo * 256, 256), 256)].reshape(768, 256)
                total += jnp.dot(rows_of(hi, h), cols, preferred_element_type=F32)
            return total[0:256], total[256:512]

        def make_crosses(hi):
            total = jnp.zeros((512, 128), F32)
            for h in range(2):
                total += jnp.dot(rows_of(hi, h), tbuf[:, h].reshape(768, 128), preferred_element_type=F32)
            for r in range(2):
                crosses[hi, r] = total[r * 256:(r + 1) * 256].T

        def crosses_of(r, index):
            return crosses[index // 2, r, pl.ds(pl.multiple_of((index % 2) * 64, 64), 64), :]

        top, low = pl.ds(0, 160), pl.ds(160, 160)

        def far_copy(r, half):
            rows = low if half else top
            return remote(xsend.at[r, 0, rows], xpass.at[r, rows], far_send.at[r, half], far_recv.at[r, half],
                          chip_x(left if half else right, 0))

        def near_copy(r, way, half):
            rows = low if half else top
            return remote(xsend.at[r, 1 + way, rows], xrecv.at[way, rows], near_send.at[r, way, half],
                          near_recv.at[way, half], chip_x(left if way else right, r))

        far = (x + 2) % 4
        make_crosses(1 - xh)
        grams = grams_of(far)
        for r in (1, 0):
            xsend[r, 0, 0:256, :] = grams[r].astype(BF16)
            xsend[r, 0, 256:320, :] = crosses_of(r, far).astype(BF16)
            start(far_copy(r, 0))
            start(far_copy(r, 1))
        make_crosses(xh)
        grams_right = grams_of(right)
        for r in (1, 0):
            xsend[r, 1, 160:256, :] = grams_right[r][160:256].astype(BF16)
            xsend[r, 1, 256:320, :] = crosses_of(r, right).astype(BF16)
            start(near_copy(r, 0, 1))
        grams_left = grams_of(left)
        for r in (1, 0):
            xsend[r, 2, 0:160, :] = grams_left[r][0:160].astype(BF16)
            start(near_copy(r, 1, 0))
        for r in (1, 0):
            far_copy(r, 0).wait_recv()
            xsend[r, 1, 0:160, :] = (grams_right[r][0:160] + xpass[r, 0:160, :].astype(F32)).astype(BF16)
            start(near_copy(r, 0, 0))
            far_copy(r, 1).wait_recv()
            xsend[r, 2, 160:256, :] = (grams_left[r][160:256] + xpass[r, 160:256, :].astype(F32)).astype(BF16)
            xsend[r, 2, 256:320, :] = (crosses_of(r, left) + xpass[r, 256:320, :].astype(F32)).astype(BF16)
            start(near_copy(r, 1, 1))
        grams = grams_of(x)
        own_block[1, 0:256, :] = grams[1]
        own_block[1, 256:320, :] = crosses_of(1, x)
        start(remote(own_block.at[1], own_block.at[0], own_send, own_recv, device(1)))
        own_block[0, 0:256, :] = grams[0]
        own_block[0, 256:320, :] = crosses_of(0, x)

        for i in range(3):
            remote(end_beta, end_beta if i == 2 else end_part.at[i], end_send.at[i], end_recv.at[i],
                   device(1)).wait_recv()
        step = step_size[0]
        product = end_part[0] + end_part[1]
        coef_out[...] = soften(end_beta[...] - step * (product - cross_state[0]), step * penalty[0])
        for copy in sent:
            copy.wait_send()

    @pl.when(c == 1)
    def _():
        remote(own_block.at[1], own_block.at[0], own_send, own_recv, device(0)).wait_recv()

    for way in range(2):
        for half in range(2):
            rows = pl.ds(160 * half, 160)
            remote(xsend.at[0, 1 + way, rows], xrecv.at[way, rows], near_send.at[0, way, half],
                   near_recv.at[way, half], chip_x(left if way else right, 0)).wait_recv()
    sums = own_block[0] + xrecv[0].astype(F32) + xrecv[1].astype(F32)
    gram_out[...] = gram_state[1] + sums[0:256] / CELLS
    cross_out[...] = cross_state[1] + sums[256:320] / CELLS


def copy_out(gram, cross, coef, gram_out, cross_out, coef_out, gram_here, cross_here, coef_here, sems_in, sems_out):
    stages = ((gram, gram_here, gram_out), (cross, cross_here, cross_out), (coef, coef_here, coef_out))
    ins = [pltpu.make_async_copy(source, here, sems_in.at[i]) for i, (source, here, _) in enumerate(stages)]
    outs = [pltpu.make_async_copy(here, out, sems_out.at[i]) for i, (_, here, out) in enumerate(stages)]
    for copy in ins:
        copy.start()
    for arrived, copy in zip(ins, outs):
        arrived.wait()
        copy.start()
    for copy in outs:
        copy.wait()


def body(expr_stretch, target_stretch, subsample, gram_state, cross_state, step_size, penalty):
    vmem = pl.BlockSpec(memory_space=pltpu.VMEM)
    hbm = pl.BlockSpec(memory_space=pltpu.HBM)
    dma = pltpu.SemaphoreType.DMA
    out_shape = (
        jax.ShapeDtypeStruct((256, 256), F32),
        jax.ShapeDtypeStruct((64, 256), F32),
        jax.ShapeDtypeStruct((64, 256), F32),
    )
    results = pl.pallas_call(
        kernel,
        out_shape=out_shape,
        in_specs=[hbm] * 7,
        out_specs=(vmem, vmem, vmem),
        scratch_shapes=[
            pltpu.VMEM((64, 384), BF16),
            pltpu.VMEM((2, CELLS), jnp.int32),
            pltpu.VMEM((2, 256, 256), F32),
            pltpu.VMEM((2, 64, 256), F32),
            pltpu.SMEM((2,), F32),
            pltpu.SMEM((2,), F32),
            pltpu.VMEM((2, RING, 256, 256), BF16),
            pltpu.VMEM((2, 2, RING, 128, 256), BF16),
            pltpu.VMEM((2, 64, 256), F32),
            pltpu.VMEM((2, 2, 64, 256), BF16),
            pltpu.VMEM((2, 2, 128, 256), F32),
            pltpu.VMEM((2, 2, 64, 256), F32),
            pltpu.VMEM((2, RING, 96, 512), BF16),
            pltpu.VMEM((RING, 2, 96, 128), BF16),
            pltpu.VMEM((RING, 768, 128), BF16),
            pltpu.VMEM((2, 2, 512, 768), BF16),
            pltpu.VMEM((384, 128), BF16),
            pltpu.VMEM((192, 128), BF16),
            pltpu.VMEM((192, 128), BF16),
            pltpu.VMEM((2, 2, 128, 256), F32),
            pltpu.VMEM((2, 2, 768), F32),
            pltpu.VMEM((256, 256), BF16),
            pltpu.VMEM((2, 3, 320, 256), BF16),
            pltpu.VMEM((2, 320, 256), BF16),
            pltpu.VMEM((2, 320, 256), F32),
            pltpu.VMEM((2, 320, 256), BF16),
            pltpu.VMEM((2, 64, 256), F32),
            pltpu.VMEM((64, 256), F32),
            pltpu.VMEM((64, 256), F32),
            dma((6, 2, 4)), dma((6, 2, 4)),
            dma((7,)), dma((7,)),
            dma((2, 2, 2)), dma((2, 2, 2)),
            dma((2, 2)), dma((2, 2)),
            dma((2, 2)), dma((2, 2)),
            dma((2, 2, 2)), dma((2, 2)),
            dma((2,)), dma((2,)),
            dma((3,)), dma((3,)),
            dma, dma,
            dma, dma,
            dma((3,)),
            dma((6,)),
        ],
        compiler_params=pltpu.CompilerParams(
            collective_id=0, has_side_effects=True, vmem_limit_bytes=60 * 2**20),
    )(
        expr_stretch,
        target_stretch.T,
        subsample,
        gram_state[:, 0],
        jnp.swapaxes(cross_state[:, 0], 1, 2),
        step_size,
        penalty,
    )
    gram, cross, coef = pl.pallas_call(
        copy_out,
        out_shape=out_shape,
        in_specs=[hbm] * 3,
        out_specs=(hbm, hbm, hbm),
        scratch_shapes=[
            pltpu.VMEM((256, 256), F32),
            pltpu.VMEM((64, 256), F32),
            pltpu.VMEM((64, 256), F32),
            dma((3,)),
            dma((3,)),
        ],
        compiler_params=pltpu.CompilerParams(vmem_limit_bytes=60 * 2**20),
    )(*results)
    return gram[None], cross.T[None], coef.T[None]


def solution(mesh):
    return jax.shard_map(
        body,
        mesh=mesh,
        in_specs=(
            P("reg", None),
            P("reg", "tgt"),
            P(),
            P(None, "grp", "reg", "tgt"),
            P(None, "grp", "reg", "tgt"),
            P(),
            P(),
        ),
        out_specs=(P("grp", "reg", "tgt"), P("grp", "reg", "tgt"), P("grp", "reg", "tgt")),
        check_vma=False,
    )
```

```python
import jax
import jax.numpy as jnp
from jax import lax
from jax.experimental import pallas as pl
from jax.experimental.pallas import tpu as pltpu
from jax.sharding import PartitionSpec as P

RING = 8
CELLS = 6144
F32, BF16 = jnp.float32, jnp.bfloat16
ROWS_T = (((1,), (1,)), ((), ()))


def soften(values, threshold):
    return values - jnp.clip(values, -threshold, threshold)


def kernel(
    expr, target_hbm, subsample_hbm, gram_hbm, cross_hbm, step_hbm, penalty_hbm,
    gram_out, cross_out, coef_out,
    target, subsample, gram_state, cross_state, step_size, penalty,
    gbuf, bbuf, cross_fit, bsend, acc, precv,
    bsend_zero, cbuf, tbuf, rbuf, lhs, tpad, tsend, trecv, crosses, wbuf, gsend,
    xsend, xpass, own_block, xrecv, end_part, end_beta, beta_keep,
    ring_send, ring_recv, spread_send, spread_recv, piece_send, piece_recv,
    part_send, part_recv, far_send, far_recv, near_send, near_recv,
    feed_send, feed_recv, end_send, end_recv, own_send, own_recv,
    swap_send, swap_recv, local_sem, load_sem, first_send, reach_send, reach_recv,
):
    c = lax.axis_index("grp")
    reg = lax.axis_index("reg")
    tgt = lax.axis_index("tgt")
    z, xh = reg // 2, reg % 2
    y, xl = tgt // 2, tgt % 2
    x = xh * 2 + xl

    def device(core, zz=z, hi=xh, yy=y, lo=xl):
        return (core, zz * 2 + hi, yy * 2 + lo)

    def chip_x(index, core):
        return device(core, hi=index // 2, lo=index % 2)

    def remote(src, dst, send, recv, to):
        return pltpu.make_async_remote_copy(
            src_ref=src, dst_ref=dst, send_sem=send, recv_sem=recv,
            device_id=to, device_id_type=pl.DeviceIdType.MESH,
        )

    right, left = (x + 1) % 4, (x + 3) % 4
    barrier = pltpu.get_barrier_semaphore()

    def greet(peers):
        for peer in peers:
            pl.semaphore_signal(barrier, inc=1, device_id=peer, device_id_type=pl.DeviceIdType.MESH)

    def load(index, source, here):
        copy = pltpu.make_async_copy(source, here, load_sem.at[index])
        copy.start()
        return copy

    def rings(core, view_of, along_y, sent):
        def ring_copy(ring, part, way, hop, chunk):
            here = y if ring in along_y else z
            there = (here + (1 if way == 0 else RING - 1)) % RING
            view = view_of(ring, part, chunk)
            slot = ring * 2 + part
            return remote(view, view, ring_send.at[slot, way, hop - 1], ring_recv.at[slot, way, hop - 1],
                          device(core, yy=there) if ring in along_y else device(core, zz=there))

        def ring_start(ring, part):
            here = y if ring in along_y else z
            for way in range(2):
                copy = ring_copy(ring, part, way, 1, here)
                copy.start()
                sent.append(copy)

        def ring_step(ring, part, hop):
            here = y if ring in along_y else z
            for way in range(2):
                if hop == 4 and way != part:
                    continue
                chunk = (here + (RING - hop if way == 0 else hop)) % RING
                ring_copy(ring, part, way, hop, chunk).wait_recv()
                if hop < 3 or (hop == 3 and way == part):
                    copy = ring_copy(ring, part, way, hop + 1, chunk)
                    copy.start()
                    sent.append(copy)

        return ring_start, ring_step

    def finish_sums():
        for way in range(2):
            for half in range(2):
                rows = pl.ds(160 * half, 160)
                remote(xsend.at[0, 1 + way, rows], xrecv.at[way, rows], near_send.at[0, way, half],
                       near_recv.at[way, half], chip_x(left if way else right, 0)).wait_recv()
        sums = own_block[0] + xrecv[0].astype(F32) + xrecv[1].astype(F32)
        gram_out[...] = gram_state[1] + sums[0:256] / CELLS
        cross_out[...] = cross_state[1] + sums[256:320] / CELLS

    @pl.when(c == 1)
    def _():
        GRAM, BETA = 0, 1
        loads = [
            load(0, step_hbm, step_size), load(1, penalty_hbm, penalty),
            load(2, cross_hbm, cross_state), load(3, gram_hbm, gram_state),
        ]
        peers = [device(1, zz=(z + d) % RING) for d in (1, 2, 6, 7)]
        peers += [device(core, yy=(y + d) % RING) for core in (0, 1) for d in (1, 7)]
        peers += [chip_x((x + d) % 4, core) for core in (0, 1) for d in (1, 2, 3)]
        peers += [device(0)]
        greet(peers)
        sent = []

        def start(copy):
            copy.start()
            sent.append(copy)

        def view_of(ring, part, chunk):
            if ring == GRAM:
                return gbuf.at[part, chunk]
            return bbuf.at[ring - BETA, part, chunk]

        ring_start, ring_step = rings(1, view_of, (GRAM,), sent)
        own_k = xl == xh

        def own_half(ref_index):
            return pl.ds(pl.multiple_of(ref_index * 64, 64), 64)

        def piece_slot(it, r, lo):
            return bbuf.at[it, r, z, own_half(lo)]

        def piece_near(it, r):
            return remote(bsend.at[it, r], piece_slot(it, r, xl), piece_send.at[it, r, 1],
                          piece_recv.at[it, r, xl], device(1, lo=1 - xl))

        def pieces_start(it, r):
            start(remote(bsend.at[it, r], piece_slot(it, r, xl), piece_send.at[it, r, 0],
                         piece_recv.at[it, r, xl], device(1, hi=1 - xh, lo=xh)))

            @pl.when(own_k)
            def _():
                pltpu.make_async_copy(
                    bsend.at[it, r], piece_slot(it, r, xl), piece_recv.at[it, r, xl]).start()

            @pl.when(jnp.logical_not(own_k))
            def _():
                piece_near(it, r).start()

        def pieces_wait(it, r):
            for lo in range(2):
                pltpu.make_async_copy(
                    bsend.at[it, r], piece_slot(it, r, lo), piece_recv.at[it, r, lo]).wait()

        def add_products(it, r, distances, first=False):
            total = None
            for distance in distances:
                k = (y + distance) % RING if it == 0 else (z + distance) % RING
                term = lax.dot_general(bbuf[it, r, k], gbuf[r, k], ROWS_T, preferred_element_type=F32)
                total = term if total is None else total + term
            acc[it, r] = total if first else acc[it, r] + total

        def part_copy(it, r):
            return remote(acc.at[it, r, own_half(1 - xl)], precv.at[it, r],
                          part_send.at[it, r], part_recv.at[it, r], device(1, lo=1 - xl))

        def step_of(r):
            return step_size[r], step_size[r] * penalty[r]

        def next_beta(it, r, beta):
            step, threshold = step_of(r)
            part_copy(it, r).wait_recv()
            product = acc[it, r, own_half(xl)] + precv[it, r]
            return soften(beta - step * (product - cross_fit[r]), threshold)

        for copy in loads:
            copy.wait()
        gbuf[1, y] = gram_state[0].astype(BF16)
        cross_fit[1] = cross_state[0]
        step, threshold = step_of(1)
        beta_one = soften(step * cross_state[0], threshold)
        bsend[0, 1] = beta_one.astype(BF16)
        pl.semaphore_wait(barrier, len(peers))

        ring_start(GRAM, 1)
        pieces_start(0, 1)
        cross_feed = remote(cross_state.at[0], cross_fit.at[0], feed_send.at[1], feed_recv.at[1], device(0))
        gram_feed = remote(gsend, gbuf.at[0, y], feed_send.at[0], feed_recv.at[0], device(0))
        for r in (1, 0):
            ring_step(GRAM, r, 1)
            pieces_wait(0, r)
            ring_start(BETA, r)
        for r in (1, 0):
            ring_step(BETA, r, 1)
        for r in (1, 0):
            ring_step(GRAM, r, 2)
        for r in (1, 0):
            ring_step(BETA, r, 2)
        for r in (1, 0):
            ring_step(GRAM, r, 3)
        for hop in (3, 4):
            for r in (1, 0):
                ring_step(BETA, r, hop)
        cross_feed.wait_recv()
        step, threshold = step_of(0)
        beta_zero = soften(step * cross_fit[0], threshold)
        gram_feed.wait_recv()
        for r in (1, 0):
            add_products(0, r, (0, 1, 2, 3, 5, 6, 7), first=True)
        for r in (1, 0):
            ring_step(GRAM, r, 4)
            add_products(0, r, (4,))
            start(part_copy(0, r))
        betas = [beta_zero, beta_one]
        for r in (1, 0):
            betas[r] = next_beta(0, r, betas[r])
            bsend[1, r] = betas[r].astype(BF16)
            pieces_start(1, r)
        beta_keep[...] = betas[0]
        start(remote(beta_keep, end_beta, end_send.at[2], end_recv.at[2], device(0)))
        def reach_copy(r, slot, chunk, to):
            view = bbuf.at[1, r, chunk % RING]
            return remote(view, view, reach_send.at[r, slot], reach_recv.at[r, slot],
                          device(1, zz=(z + to) % RING))

        M1, P1, M2, P2, M3, P3, FAR = range(7)
        for r in (1, 0):
            pieces_wait(1, r)
            start(reach_copy(r, M2, z, 2))
            start(reach_copy(r, P2, z, 6))
            start(reach_copy(r, M1, z, 1))
            start(reach_copy(r, P1, z, 7))
        for r in (1, 0):
            add_products(1, r, (0,), first=True)
        for r in (1, 0):
            reach_copy(r, M2, z + 6, 2).wait_recv()
            start(reach_copy(r, M3, z + 6, 1))
            if r == 0:
                start(reach_copy(r, FAR, z + 6, 2))
            reach_copy(r, P2, z + 2, 6).wait_recv()
            start(reach_copy(r, P3, z + 2, 7))
            if r == 1:
                start(reach_copy(r, FAR, z + 2, 6))
        for r in (1, 0):
            reach_copy(r, M1, z + 7, 1).wait_recv()
            reach_copy(r, P1, z + 1, 7).wait_recv()
            add_products(1, r, (1, 2, 6, 7))

        def last_products(r):
            reach_copy(r, M3, z + 5, 1).wait_recv()
            reach_copy(r, P3, z + 3, 7).wait_recv()
            reach_copy(r, FAR, z + 4, 2).wait_recv()
            add_products(1, r, (3, 4, 5))

        last_products(1)
        start(part_copy(1, 1))
        last_products(0)
        start(remote(acc.at[1, 0, own_half(1 - xl)], end_part.at[1], end_send.at[1], end_recv.at[1],
                     device(0, lo=1 - xl)))
        start(remote(acc.at[1, 0, own_half(xl)], end_part.at[0], end_send.at[0], end_recv.at[0], device(0)))
        remote(own_block.at[1], own_block.at[0], own_send, own_recv, device(0)).wait_recv()
        finish_sums()
        coef_out[...] = next_beta(1, 1, betas[1])

        for copy in sent:
            copy.wait_send()
        for it, r in ((0, 1), (1, 0), (1, 1)):
            @pl.when(jnp.logical_not(own_k))
            def _():
                piece_near(it, r).wait_send()

    @pl.when(c == 0)
    def _():
        COLS, ROWS, TARGETS = 0, 1, 2
        row0 = pl.multiple_of(xl * 192, 16)
        row0_other = pl.multiple_of((1 - xl) * 192, 16)
        part_h, part_q = y // 4, y % 4
        rows_h = pl.multiple_of(xl * 192 + part_h * 96, 16)

        def at96(index):
            return pl.ds(pl.multiple_of(index * 96, 16), 96)

        def expr_cols(index):
            return pl.ds(pl.multiple_of(index * 512 + part_q * 128, 128), 128)

        loads = [
            load(0, step_hbm, step_size), load(1, penalty_hbm, penalty), load(2, cross_hbm, cross_state),
            load(3, gram_hbm, gram_state), load(4, target_hbm, target), load(5, subsample_hbm, subsample),
        ]
        peers = [device(0, zz=(z + d) % RING) for d in range(1, RING)]
        peers += [device(core, yy=(y + d) % RING) for core in (0, 1) for d in (1, 7)]
        peers += [chip_x(right, 0), chip_x(left, 0), device(1)]
        peers += [chip_x((x + d) % 4, 1) for d in (1, 2, 3)]
        greet(peers)
        local = [
            pltpu.make_async_copy(
                expr.at[pl.ds(pl.multiple_of(row0 + h * 96, 16), 96), pl.ds(pl.multiple_of(y * 512, 512), 512)],
                cbuf.at[h, z], local_sem.at[h])
            for h in range(2)
        ]
        local.append(pltpu.make_async_copy(
            expr.at[pl.ds(rows_h, 96), expr_cols(z)], rbuf.at[y, at96(z)], local_sem.at[2]))
        for copy in local:
            copy.start()
        sent = []

        def start(copy):
            copy.start()
            sent.append(copy)

        def view_of(ring, part, chunk):
            if ring == COLS:
                return cbuf.at[part, chunk]
            if ring == TARGETS:
                return tbuf.at[chunk]
            return rbuf.at[chunk, pl.ds(part * 384, 384)]

        ring_start, ring_step = rings(0, view_of, (ROWS,), sent)

        for copy in loads[:4]:
            copy.wait()
        gsend[...] = gram_state[0].astype(BF16)
        step = step_size[0]
        threshold = step * penalty[0]
        bsend_zero[...] = soften(step * cross_state[0], threshold).astype(BF16)
        loads[4].wait()
        both = jnp.concatenate([target[...], target[...]], axis=0)
        lane_half = lax.broadcasted_iota(jnp.int32, both.shape, 0) // 64
        both = jnp.where(lane_half == xl, both, jnp.zeros_like(both))
        tpad[...] = both.T
        tsend[...] = tpad[pl.ds(row0_other, 192), :]
        pl.semaphore_wait(barrier, len(peers))

        for way in range(2):
            start(remote(gsend, gbuf.at[0, y], first_send.at[way], ring_recv.at[0, way, 0],
                         device(1, yy=(y + (7 if way else 1)) % RING)))
        for i, hi in enumerate((1 - xh, xh)):
            start(remote(bsend_zero, bbuf.at[0, 0, z, pl.ds(pl.multiple_of(xl * 64, 64), 64)], first_send.at[2 + i],
                         piece_recv.at[0, 0, xl], device(1, hi=hi, lo=xh)))
        start(remote(gsend, gbuf.at[0, y], feed_send.at[0], feed_recv.at[0], device(1)))
        start(remote(cross_state.at[0], cross_fit.at[0], feed_send.at[1], feed_recv.at[1], device(1)))
        swap = remote(tsend, trecv, swap_send, swap_recv, device(0, lo=1 - xl))
        start(swap)
        for d in range(1, RING):
            to = (z + d) % RING
            start(remote(expr.at[pl.ds(rows_h, 96), expr_cols(to)], rbuf.at[y, at96(z)],
                         spread_send.at[d - 1], spread_recv.at[d - 1], device(0, zz=to)))
        for copy in local:
            copy.wait()
        for part in range(2):
            ring_start(COLS, part)
        swap.wait_recv()
        for h in range(2):
            tbuf[z, h] = (
                tpad[pl.ds(pl.multiple_of(row0 + h * 96, 16), 96), :] + trecv[h * 96:(h + 1) * 96, :])
        ring_start(TARGETS, 0)
        for d in range(1, RING):
            source = (z + RING - d) % RING
            remote(expr.at[pl.ds(rows_h, 96), expr_cols(z)], rbuf.at[y, at96(source)],
                   spread_send.at[d - 1], spread_recv.at[d - 1], device(0, zz=source)).wait_recv()
        for part in range(2):
            ring_start(ROWS, part)

        loads[5].wait()
        first_lane = xh * 384 + xl * 192
        lane = lax.broadcasted_iota(jnp.int32, (2, 768), 1)
        for h in range(2):
            weights = jnp.zeros((2, 768), F32)
            for zz in range(RING):
                cells = subsample[:, zz * 768:(zz + 1) * 768].astype(F32)
                moved = pltpu.roll(cells, (1536 + zz * 96 - h * 96 - first_lane) % 768, axis=1)
                weights = jnp.where((lane >= zz * 96) & (lane < zz * 96 + 96), moved, weights)
            wbuf[h] = weights

        def weigh(distance):
            chunk = (y + distance) % RING
            h, q = chunk // 4, chunk % 4
            block = rbuf[chunk].T
            rows = pl.ds(pl.multiple_of(q * 128, 128), 128)
            pair = wbuf[h].astype(BF16)
            for r in range(2):
                lhs[r, h, rows, :] = block * pair[r:r + 1, :]

        weigh(0)
        for hop in (1, 2, 3):
            for part in range(2):
                ring_step(ROWS, part, hop)
            for part in range(2):
                ring_step(COLS, part, hop)
            ring_step(TARGETS, 0, hop)
            weigh(hop)
            weigh(RING - hop)
        for part in range(2):
            ring_step(COLS, part, 4)
        ring_step(TARGETS, 0, 4)
        for part in range(2):
            ring_step(ROWS, part, 4)
        weigh(4)

        def rows_of(hi, h):
            half = pl.ds(pl.multiple_of(hi * 256, 256), 256)
            return jnp.concatenate([lhs[0, h, half, :], lhs[1, h, half, :]], axis=0)

        def grams_of(index):
            hi, lo = index // 2, index % 2
            total = jnp.zeros((512, 256), F32)
            for h in range(2):
                cols = cbuf[h, :, :, pl.ds(pl.multiple_of(lo * 256, 256), 256)].reshape(768, 256)
                total += jnp.dot(rows_of(hi, h), cols, preferred_element_type=F32)
            return total[0:256], total[256:512]

        def make_crosses(hi):
            total = jnp.zeros((512, 128), F32)
            for h in range(2):
                total += jnp.dot(rows_of(hi, h), tbuf[:, h].reshape(768, 128), preferred_element_type=F32)
            for r in range(2):
                crosses[hi, r] = total[r * 256:(r + 1) * 256].T

        def crosses_of(r, index):
            return crosses[index // 2, r, pl.ds(pl.multiple_of((index % 2) * 64, 64), 64), :]

        top, low = pl.ds(0, 160), pl.ds(160, 160)

        def far_copy(r, half):
            rows = low if half else top
            return remote(xsend.at[r, 0, rows], xpass.at[r, rows], far_send.at[r, half], far_recv.at[r, half],
                          chip_x(left if half else right, 0))

        def near_copy(r, way, half):
            rows = low if half else top
            return remote(xsend.at[r, 1 + way, rows], xrecv.at[way, rows], near_send.at[r, way, half],
                          near_recv.at[way, half], chip_x(left if way else right, r))

        far = (x + 2) % 4
        make_crosses(1 - xh)
        grams = grams_of(far)
        for r in (1, 0):
            xsend[r, 0, 0:256, :] = grams[r].astype(BF16)
            xsend[r, 0, 256:320, :] = crosses_of(r, far).astype(BF16)
            start(far_copy(r, 0))
            start(far_copy(r, 1))
        make_crosses(xh)
        grams_right = grams_of(right)
        for r in (1, 0):
            xsend[r, 1, 160:256, :] = grams_right[r][160:256].astype(BF16)
            xsend[r, 1, 256:320, :] = crosses_of(r, right).astype(BF16)
            start(near_copy(r, 0, 1))
        grams_left = grams_of(left)
        for r in (1, 0):
            xsend[r, 2, 0:160, :] = grams_left[r][0:160].astype(BF16)
            start(near_copy(r, 1, 0))
        for r in (1, 0):
            far_copy(r, 0).wait_recv()
            xsend[r, 1, 0:160, :] = (grams_right[r][0:160] + xpass[r, 0:160, :].astype(F32)).astype(BF16)
            start(near_copy(r, 0, 0))
            far_copy(r, 1).wait_recv()
            xsend[r, 2, 160:256, :] = (grams_left[r][160:256] + xpass[r, 160:256, :].astype(F32)).astype(BF16)
            xsend[r, 2, 256:320, :] = (crosses_of(r, left) + xpass[r, 256:320, :].astype(F32)).astype(BF16)
            start(near_copy(r, 1, 1))
        grams = grams_of(x)
        own_block[1, 0:256, :] = grams[1]
        own_block[1, 256:320, :] = crosses_of(1, x)
        start(remote(own_block.at[1], own_block.at[0], own_send, own_recv, device(1)))
        own_block[0, 0:256, :] = grams[0]
        own_block[0, 256:320, :] = crosses_of(0, x)

        finish_sums()
        for i in range(3):
            remote(end_beta, end_beta if i == 2 else end_part.at[i], end_send.at[i], end_recv.at[i],
                   device(1)).wait_recv()
        product = end_part[0] + end_part[1]
        coef_out[...] = soften(end_beta[...] - step * (product - cross_state[0]), threshold)
        for copy in sent:
            copy.wait_send()


def copy_out(gram, cross, coef, gram_out, cross_out, coef_out, gram_here, cross_here, coef_here, sems_in, sems_out):
    stages = ((gram, gram_here, gram_out), (cross, cross_here, cross_out), (coef, coef_here, coef_out))
    ins = [pltpu.make_async_copy(source, here, sems_in.at[i]) for i, (source, here, _) in enumerate(stages)]
    outs = [pltpu.make_async_copy(here, out, sems_out.at[i]) for i, (_, here, out) in enumerate(stages)]
    for copy in ins:
        copy.start()
    for arrived, copy in zip(ins, outs):
        arrived.wait()
        copy.start()
    for copy in outs:
        copy.wait()


def body(expr_stretch, target_stretch, subsample, gram_state, cross_state, step_size, penalty):
    vmem = pl.BlockSpec(memory_space=pltpu.VMEM)
    hbm = pl.BlockSpec(memory_space=pltpu.HBM)
    dma = pltpu.SemaphoreType.DMA
    out_shape = (
        jax.ShapeDtypeStruct((256, 256), F32),
        jax.ShapeDtypeStruct((64, 256), F32),
        jax.ShapeDtypeStruct((64, 256), F32),
    )
    results = pl.pallas_call(
        kernel,
        out_shape=out_shape,
        in_specs=[hbm] * 7,
        out_specs=(vmem, vmem, vmem),
        scratch_shapes=[
            pltpu.VMEM((64, 384), BF16),
            pltpu.VMEM((2, CELLS), jnp.int32),
            pltpu.VMEM((2, 256, 256), F32),
            pltpu.VMEM((2, 64, 256), F32),
            pltpu.SMEM((2,), F32),
            pltpu.SMEM((2,), F32),
            pltpu.VMEM((2, RING, 256, 256), BF16),
            pltpu.VMEM((2, 2, RING, 128, 256), BF16),
            pltpu.VMEM((2, 64, 256), F32),
            pltpu.VMEM((2, 2, 64, 256), BF16),
            pltpu.VMEM((2, 2, 128, 256), F32),
            pltpu.VMEM((2, 2, 64, 256), F32),
            pltpu.VMEM((64, 256), BF16),
            pltpu.VMEM((2, RING, 96, 512), BF16),
            pltpu.VMEM((RING, 2, 96, 128), BF16),
            pltpu.VMEM((RING, 768, 128), BF16),
            pltpu.VMEM((2, 2, 512, 768), BF16),
            pltpu.VMEM((384, 128), BF16),
            pltpu.VMEM((192, 128), BF16),
            pltpu.VMEM((192, 128), BF16),
            pltpu.VMEM((2, 2, 128, 256), F32),
            pltpu.VMEM((2, 2, 768), F32),
            pltpu.VMEM((256, 256), BF16),
            pltpu.VMEM((2, 3, 320, 256), BF16),
            pltpu.VMEM((2, 320, 256), BF16),
            pltpu.VMEM((2, 320, 256), F32),
            pltpu.VMEM((2, 320, 256), BF16),
            pltpu.VMEM((2, 64, 256), F32),
            pltpu.VMEM((64, 256), F32),
            pltpu.VMEM((64, 256), F32),
            dma((6, 2, 4)), dma((6, 2, 4)),
            dma((7,)), dma((7,)),
            dma((2, 2, 2)), dma((2, 2, 2)),
            dma((2, 2)), dma((2, 2)),
            dma((2, 2)), dma((2, 2)),
            dma((2, 2, 2)), dma((2, 2)),
            dma((2,)), dma((2,)),
            dma((3,)), dma((3,)),
            dma, dma,
            dma, dma,
            dma((3,)),
            dma((6,)),
            dma((4,)),
            dma((2, 7)), dma((2, 7)),
        ],
        compiler_params=pltpu.CompilerParams(
            collective_id=0, has_side_effects=True, vmem_limit_bytes=60 * 2**20),
    )(
        expr_stretch,
        target_stretch.T,
        subsample,
        gram_state[:, 0],
        jnp.swapaxes(cross_state[:, 0], 1, 2),
        step_size,
        penalty,
    )
    gram, cross, coef = pl.pallas_call(
        copy_out,
        out_shape=out_shape,
        in_specs=[hbm] * 3,
        out_specs=(hbm, hbm, hbm),
        scratch_shapes=[
            pltpu.VMEM((256, 256), F32),
            pltpu.VMEM((64, 256), F32),
            pltpu.VMEM((64, 256), F32),
            dma((3,)),
            dma((3,)),
        ],
        compiler_params=pltpu.CompilerParams(vmem_limit_bytes=60 * 2**20),
    )(*results)
    return gram[None], cross.T[None], coef.T[None]


def solution(mesh):
    return jax.shard_map(
        body,
        mesh=mesh,
        in_specs=(
            P("reg", None),
            P("reg", "tgt"),
            P(),
            P(None, "grp", "reg", "tgt"),
            P(None, "grp", "reg", "tgt"),
            P(),
            P(),
        ),
        out_specs=(P("grp", "reg", "tgt"), P("grp", "reg", "tgt"), P("grp", "reg", "tgt")),
        check_vma=False,
    )
```

```python
import jax
import jax.numpy as jnp
from jax import lax
from jax.experimental import pallas as pl
from jax.experimental.pallas import tpu as pltpu
from jax.sharding import PartitionSpec as P

RING = 8
CELLS = 6144
F32, BF16 = jnp.float32, jnp.bfloat16
ROWS_T = (((1,), (1,)), ((), ()))


def soften(values, threshold):
    return values - jnp.clip(values, -threshold, threshold)


def kernel(
    expr, target_hbm, subsample_hbm, gram_hbm, cross_hbm, step_hbm, penalty_hbm,
    gram_out, cross_out, coef_out,
    target, subsample, gram_state, cross_state, step_size, penalty,
    gbuf, bbuf, cross_fit, bsend, acc, precv,
    bsend_zero, stage, cbuf, tbuf, rbuf, lhs, tpad, tsend, trecv, crosses, wbuf, gsend,
    xsend, xpass, own_block, xrecv, end_part, end_beta, beta_keep,
    ring_send, ring_recv, spread_send, spread_recv, piece_send, piece_recv,
    part_send, part_recv, far_send, far_recv, near_send, near_recv,
    feed_send, feed_recv, end_send, end_recv, own_send, own_recv,
    swap_send, swap_recv, local_sem, load_sem, stage_sem, first_send, reach_send, reach_recv,
):
    c = lax.axis_index("grp")
    reg = lax.axis_index("reg")
    tgt = lax.axis_index("tgt")
    z, xh = reg // 2, reg % 2
    y, xl = tgt // 2, tgt % 2
    x = xh * 2 + xl

    def device(core, zz=z, hi=xh, yy=y, lo=xl):
        return (core, zz * 2 + hi, yy * 2 + lo)

    def chip_x(index, core):
        return device(core, hi=index // 2, lo=index % 2)

    def remote(src, dst, send, recv, to):
        return pltpu.make_async_remote_copy(
            src_ref=src, dst_ref=dst, send_sem=send, recv_sem=recv,
            device_id=to, device_id_type=pl.DeviceIdType.MESH,
        )

    right, left = (x + 1) % 4, (x + 3) % 4
    barrier = pltpu.get_barrier_semaphore()

    def greet(peers):
        for peer in peers:
            pl.semaphore_signal(barrier, inc=1, device_id=peer, device_id_type=pl.DeviceIdType.MESH)

    def load(index, source, here):
        copy = pltpu.make_async_copy(source, here, load_sem.at[index])
        copy.start()
        return copy

    def rings(core, view_of, along_y, sent):
        def ring_copy(ring, part, way, hop, chunk):
            here = y if ring in along_y else z
            there = (here + (1 if way == 0 else RING - 1)) % RING
            view = view_of(ring, part, chunk)
            slot = ring * 2 + part
            return remote(view, view, ring_send.at[slot, way, hop - 1], ring_recv.at[slot, way, hop - 1],
                          device(core, yy=there) if ring in along_y else device(core, zz=there))

        def ring_start(ring, part):
            here = y if ring in along_y else z
            for way in range(2):
                copy = ring_copy(ring, part, way, 1, here)
                copy.start()
                sent.append(copy)

        def ring_step(ring, part, hop):
            here = y if ring in along_y else z
            for way in range(2):
                if hop == 4 and way != part:
                    continue
                chunk = (here + (RING - hop if way == 0 else hop)) % RING
                ring_copy(ring, part, way, hop, chunk).wait_recv()
                if hop < 3 or (hop == 3 and way == part):
                    copy = ring_copy(ring, part, way, hop + 1, chunk)
                    copy.start()
                    sent.append(copy)

        return ring_start, ring_step

    def finish_sums():
        for way in range(2):
            for half in range(2):
                rows = pl.ds(160 * half, 160)
                remote(xsend.at[0, 1 + way, rows], xrecv.at[way, rows], near_send.at[0, way, half],
                       near_recv.at[way, half], chip_x(left if way else right, 0)).wait_recv()
        sums = own_block[0] + xrecv[0].astype(F32) + xrecv[1].astype(F32)
        gram_out[...] = gram_state[1] + sums[0:256] / CELLS
        cross_out[...] = cross_state[1] + sums[256:320] / CELLS

    @pl.when(c == 1)
    def _():
        GRAM, BETA = 0, 1
        loads = [
            load(0, step_hbm, step_size), load(1, penalty_hbm, penalty),
            load(2, cross_hbm, cross_state), load(3, gram_hbm, gram_state),
        ]
        peers = [device(1, zz=(z + d) % RING) for d in (1, 2, 6, 7)]
        peers += [device(core, yy=(y + d) % RING) for core in (0, 1) for d in (1, 7)]
        peers += [chip_x((x + d) % 4, core) for core in (0, 1) for d in (1, 2, 3)]
        peers += [device(0)]
        greet(peers)
        sent = []

        def start(copy):
            copy.start()
            sent.append(copy)

        def view_of(ring, part, chunk):
            if ring == GRAM:
                return gbuf.at[part, chunk]
            return bbuf.at[ring - BETA, part, chunk]

        ring_start, ring_step = rings(1, view_of, (GRAM,), sent)
        own_k = xl == xh

        def own_half(ref_index):
            return pl.ds(pl.multiple_of(ref_index * 64, 64), 64)

        def piece_slot(it, r, lo):
            return bbuf.at[it, r, z, own_half(lo)]

        def piece_near(it, r):
            return remote(bsend.at[it, r], piece_slot(it, r, xl), piece_send.at[it, r, 1],
                          piece_recv.at[it, r, xl], device(1, lo=1 - xl))

        def pieces_start(it, r):
            start(remote(bsend.at[it, r], piece_slot(it, r, xl), piece_send.at[it, r, 0],
                         piece_recv.at[it, r, xl], device(1, hi=1 - xh, lo=xh)))

            @pl.when(own_k)
            def _():
                pltpu.make_async_copy(
                    bsend.at[it, r], piece_slot(it, r, xl), piece_recv.at[it, r, xl]).start()

            @pl.when(jnp.logical_not(own_k))
            def _():
                piece_near(it, r).start()

        def pieces_wait(it, r):
            for lo in range(2):
                pltpu.make_async_copy(
                    bsend.at[it, r], piece_slot(it, r, lo), piece_recv.at[it, r, lo]).wait()

        def add_products(it, r, distances, first=False):
            total = None
            for distance in distances:
                k = (y + distance) % RING if it == 0 else (z + distance) % RING
                term = lax.dot_general(bbuf[it, r, k], gbuf[r, k], ROWS_T, preferred_element_type=F32)
                total = term if total is None else total + term
            acc[it, r] = total if first else acc[it, r] + total

        def part_copy(it, r):
            return remote(acc.at[it, r, own_half(1 - xl)], precv.at[it, r],
                          part_send.at[it, r], part_recv.at[it, r], device(1, lo=1 - xl))

        def step_of(r):
            return step_size[r], step_size[r] * penalty[r]

        def next_beta(it, r, beta):
            step, threshold = step_of(r)
            part_copy(it, r).wait_recv()
            product = acc[it, r, own_half(xl)] + precv[it, r]
            return soften(beta - step * (product - cross_fit[r]), threshold)

        for copy in loads:
            copy.wait()
        gbuf[1, y] = gram_state[0].astype(BF16)
        cross_fit[1] = cross_state[0]
        step, threshold = step_of(1)
        beta_one = soften(step * cross_state[0], threshold)
        bsend[0, 1] = beta_one.astype(BF16)
        pl.semaphore_wait(barrier, len(peers))

        ring_start(GRAM, 1)
        pieces_start(0, 1)
        cross_feed = remote(cross_state.at[0], cross_fit.at[0], feed_send.at[1], feed_recv.at[1], device(0))
        gram_feed = remote(gsend, gbuf.at[0, y], feed_send.at[0], feed_recv.at[0], device(0))
        for r in (1, 0):
            ring_step(GRAM, r, 1)
            pieces_wait(0, r)
            ring_start(BETA, r)
        for r in (1, 0):
            ring_step(BETA, r, 1)
        for r in (1, 0):
            ring_step(GRAM, r, 2)
        for r in (1, 0):
            ring_step(BETA, r, 2)
        for r in (1, 0):
            ring_step(GRAM, r, 3)
        for hop in (3, 4):
            for r in (1, 0):
                ring_step(BETA, r, hop)
        cross_feed.wait_recv()
        step, threshold = step_of(0)
        beta_zero = soften(step * cross_fit[0], threshold)
        gram_feed.wait_recv()
        for r in (1, 0):
            add_products(0, r, (0, 1, 2, 3, 5, 6, 7), first=True)
        for r in (1, 0):
            ring_step(GRAM, r, 4)
            add_products(0, r, (4,))
            start(part_copy(0, r))
        betas = [beta_zero, beta_one]
        for r in (1, 0):
            betas[r] = next_beta(0, r, betas[r])
            bsend[1, r] = betas[r].astype(BF16)
            pieces_start(1, r)
        beta_keep[...] = betas[0]
        start(remote(beta_keep, end_beta, end_send.at[2], end_recv.at[2], device(0)))
        def reach_copy(r, slot, chunk, to):
            view = bbuf.at[1, r, chunk % RING]
            return remote(view, view, reach_send.at[r, slot], reach_recv.at[r, slot],
                          device(1, zz=(z + to) % RING))

        M1, P1, M2, P2, M3, P3, FAR = range(7)
        for r in (1, 0):
            pieces_wait(1, r)
            start(reach_copy(r, M2, z, 2))
            start(reach_copy(r, P2, z, 6))
            start(reach_copy(r, M1, z, 1))
            start(reach_copy(r, P1, z, 7))
        for r in (1, 0):
            add_products(1, r, (0,), first=True)
        for r in (1, 0):
            reach_copy(r, M2, z + 6, 2).wait_recv()
            start(reach_copy(r, M3, z + 6, 1))
            if r == 0:
                start(reach_copy(r, FAR, z + 6, 2))
            reach_copy(r, P2, z + 2, 6).wait_recv()
            start(reach_copy(r, P3, z + 2, 7))
            if r == 1:
                start(reach_copy(r, FAR, z + 2, 6))
        for r in (1, 0):
            reach_copy(r, M1, z + 7, 1).wait_recv()
            reach_copy(r, P1, z + 1, 7).wait_recv()
            add_products(1, r, (1, 2, 6, 7))

        def last_products(r):
            reach_copy(r, M3, z + 5, 1).wait_recv()
            reach_copy(r, P3, z + 3, 7).wait_recv()
            reach_copy(r, FAR, z + 4, 2).wait_recv()
            add_products(1, r, (3, 4, 5))

        last_products(1)
        start(part_copy(1, 1))
        last_products(0)
        start(remote(acc.at[1, 0, own_half(1 - xl)], end_part.at[1], end_send.at[1], end_recv.at[1],
                     device(0, lo=1 - xl)))
        start(remote(acc.at[1, 0, own_half(xl)], end_part.at[0], end_send.at[0], end_recv.at[0], device(0)))
        remote(own_block.at[1], own_block.at[0], own_send, own_recv, device(0)).wait_recv()
        finish_sums()
        coef_out[...] = next_beta(1, 1, betas[1])

        for copy in sent:
            copy.wait_send()
        for it, r in ((0, 1), (1, 0), (1, 1)):
            @pl.when(jnp.logical_not(own_k))
            def _():
                piece_near(it, r).wait_send()

    @pl.when(c == 0)
    def _():
        COLS, ROWS, TARGETS = 0, 1, 2
        row0 = pl.multiple_of(xl * 192, 16)
        row0_other = pl.multiple_of((1 - xl) * 192, 16)
        part_h, part_q = y // 4, y % 4
        rows_h = pl.multiple_of(xl * 192 + part_h * 96, 16)

        def at96(index):
            return pl.ds(pl.multiple_of(index * 96, 16), 96)

        def expr_cols(index):
            return pl.ds(pl.multiple_of(index * 512 + part_q * 128, 128), 128)

        peers = [device(0, zz=(z + d) % RING) for d in range(1, RING)]
        peers += [device(core, yy=(y + d) % RING) for core in (0, 1) for d in (1, 7)]
        peers += [chip_x(right, 0), chip_x(left, 0), device(1)]
        peers += [chip_x((x + d) % 4, 1) for d in (1, 2, 3)]
        greet(peers)
        loads = [
            load(0, step_hbm, step_size), load(1, penalty_hbm, penalty), load(2, cross_hbm, cross_state),
            load(3, gram_hbm, gram_state),
        ]
        stages = [
            pltpu.make_async_copy(expr.at[pl.ds(rows_h, 96), expr_cols((z + d) % RING)], stage.at[d], stage_sem.at[d])
            for d in range(1, RING)
        ]
        for copy in stages:
            copy.start()
        local = [
            pltpu.make_async_copy(
                expr.at[pl.ds(pl.multiple_of(row0 + h * 96, 16), 96), pl.ds(pl.multiple_of(y * 512, 512), 512)],
                cbuf.at[h, z], local_sem.at[h])
            for h in range(2)
        ]
        local.append(pltpu.make_async_copy(
            expr.at[pl.ds(rows_h, 96), expr_cols(z)], rbuf.at[y, at96(z)], local_sem.at[2]))
        for copy in local:
            copy.start()
        loads += [load(4, target_hbm, target), load(5, subsample_hbm, subsample)]
        sent = []

        def start(copy):
            copy.start()
            sent.append(copy)

        def view_of(ring, part, chunk):
            if ring == COLS:
                return cbuf.at[part, chunk]
            if ring == TARGETS:
                return tbuf.at[chunk]
            return rbuf.at[chunk, pl.ds(part * 384, 384)]

        ring_start, ring_step = rings(0, view_of, (ROWS,), sent)

        for copy in loads[:4]:
            copy.wait()
        gsend[...] = gram_state[0].astype(BF16)
        step = step_size[0]
        threshold = step * penalty[0]
        bsend_zero[...] = soften(step * cross_state[0], threshold).astype(BF16)
        pl.semaphore_wait(barrier, len(peers))

        for way in range(2):
            start(remote(gsend, gbuf.at[0, y], first_send.at[way], ring_recv.at[0, way, 0],
                         device(1, yy=(y + (7 if way else 1)) % RING)))
        for i, hi in enumerate((1 - xh, xh)):
            start(remote(bsend_zero, bbuf.at[0, 0, z, pl.ds(pl.multiple_of(xl * 64, 64), 64)], first_send.at[2 + i],
                         piece_recv.at[0, 0, xl], device(1, hi=hi, lo=xh)))
        for d in range(1, RING):
            stages[d - 1].wait()
            start(remote(stage.at[d], rbuf.at[y, at96(z)], spread_send.at[d - 1], spread_recv.at[d - 1],
                         device(0, zz=(z + d) % RING)))
        for copy in local:
            copy.wait()
        for part in range(2):
            ring_start(COLS, part)
        start(remote(gsend, gbuf.at[0, y], feed_send.at[0], feed_recv.at[0], device(1)))
        start(remote(cross_state.at[0], cross_fit.at[0], feed_send.at[1], feed_recv.at[1], device(1)))
        loads[4].wait()
        both = jnp.concatenate([target[...], target[...]], axis=0)
        lane_half = lax.broadcasted_iota(jnp.int32, both.shape, 0) // 64
        both = jnp.where(lane_half == xl, both, jnp.zeros_like(both))
        tpad[...] = both.T
        tsend[...] = tpad[pl.ds(row0_other, 192), :]
        swap = remote(tsend, trecv, swap_send, swap_recv, device(0, lo=1 - xl))
        start(swap)
        for d in range(1, RING):
            source = (z + RING - d) % RING
            remote(stage.at[d], rbuf.at[y, at96(source)],
                   spread_send.at[d - 1], spread_recv.at[d - 1], device(0, zz=source)).wait_recv()
        for part in range(2):
            ring_start(ROWS, part)
        swap.wait_recv()
        for h in range(2):
            tbuf[z, h] = (
                tpad[pl.ds(pl.multiple_of(row0 + h * 96, 16), 96), :] + trecv[h * 96:(h + 1) * 96, :])
        ring_start(TARGETS, 0)

        loads[5].wait()
        first_lane = xh * 384 + xl * 192
        lane = lax.broadcasted_iota(jnp.int32, (2, 768), 1)
        for h in range(2):
            weights = jnp.zeros((2, 768), F32)
            for zz in range(RING):
                cells = subsample[:, zz * 768:(zz + 1) * 768].astype(F32)
                moved = pltpu.roll(cells, (1536 + zz * 96 - h * 96 - first_lane) % 768, axis=1)
                weights = jnp.where((lane >= zz * 96) & (lane < zz * 96 + 96), moved, weights)
            wbuf[h] = weights

        def weigh(distance):
            chunk = (y + distance) % RING
            h, q = chunk // 4, chunk % 4
            block = rbuf[chunk].T
            rows = pl.ds(pl.multiple_of(q * 128, 128), 128)
            pair = wbuf[h].astype(BF16)
            for r in range(2):
                lhs[r, h, rows, :] = block * pair[r:r + 1, :]

        weigh(0)
        for hop in (1, 2, 3):
            for part in range(2):
                ring_step(ROWS, part, hop)
            for part in range(2):
                ring_step(COLS, part, hop)
            ring_step(TARGETS, 0, hop)
            weigh(hop)
            weigh(RING - hop)
        for part in range(2):
            ring_step(COLS, part, 4)
        ring_step(TARGETS, 0, 4)
        for part in range(2):
            ring_step(ROWS, part, 4)
        weigh(4)

        def rows_of(hi, h):
            half = pl.ds(pl.multiple_of(hi * 256, 256), 256)
            return jnp.concatenate([lhs[0, h, half, :], lhs[1, h, half, :]], axis=0)

        def grams_of(index):
            hi, lo = index // 2, index % 2
            total = jnp.zeros((512, 256), F32)
            for h in range(2):
                cols = cbuf[h, :, :, pl.ds(pl.multiple_of(lo * 256, 256), 256)].reshape(768, 256)
                total += jnp.dot(rows_of(hi, h), cols, preferred_element_type=F32)
            return total[0:256], total[256:512]

        def make_crosses(hi):
            total = jnp.zeros((512, 128), F32)
            for h in range(2):
                total += jnp.dot(rows_of(hi, h), tbuf[:, h].reshape(768, 128), preferred_element_type=F32)
            for r in range(2):
                crosses[hi, r] = total[r * 256:(r + 1) * 256].T

        def crosses_of(r, index):
            return crosses[index // 2, r, pl.ds(pl.multiple_of((index % 2) * 64, 64), 64), :]

        top, low = pl.ds(0, 160), pl.ds(160, 160)

        def far_copy(r, half):
            rows = low if half else top
            return remote(xsend.at[r, 0, rows], xpass.at[r, rows], far_send.at[r, half], far_recv.at[r, half],
                          chip_x(left if half else right, 0))

        def near_copy(r, way, half):
            rows = low if half else top
            return remote(xsend.at[r, 1 + way, rows], xrecv.at[way, rows], near_send.at[r, way, half],
                          near_recv.at[way, half], chip_x(left if way else right, r))

        far = (x + 2) % 4
        make_crosses(1 - xh)
        for r in (1, 0):
            gram = jnp.zeros((256, 256), F32)
            for h in range(2):
                rows = lhs[r, h, pl.ds(pl.multiple_of((1 - xh) * 256, 256), 256), :]
                cols = cbuf[h, :, :, pl.ds(pl.multiple_of(xl * 256, 256), 256)].reshape(768, 256)
                gram += jnp.dot(rows, cols, preferred_element_type=F32)
            xsend[r, 0, 0:256, :] = gram.astype(BF16)
            xsend[r, 0, 256:320, :] = crosses_of(r, far).astype(BF16)
            start(far_copy(r, 0))
            start(far_copy(r, 1))
        make_crosses(xh)
        grams_right = grams_of(right)
        for r in (1, 0):
            xsend[r, 1, 160:256, :] = grams_right[r][160:256].astype(BF16)
            xsend[r, 1, 256:320, :] = crosses_of(r, right).astype(BF16)
            start(near_copy(r, 0, 1))
        grams_left = grams_of(left)
        for r in (1, 0):
            xsend[r, 2, 0:160, :] = grams_left[r][0:160].astype(BF16)
            start(near_copy(r, 1, 0))
        for r in (1, 0):
            far_copy(r, 0).wait_recv()
            xsend[r, 1, 0:160, :] = (grams_right[r][0:160] + xpass[r, 0:160, :].astype(F32)).astype(BF16)
            start(near_copy(r, 0, 0))
            far_copy(r, 1).wait_recv()
            xsend[r, 2, 160:256, :] = (grams_left[r][160:256] + xpass[r, 160:256, :].astype(F32)).astype(BF16)
            xsend[r, 2, 256:320, :] = (crosses_of(r, left) + xpass[r, 256:320, :].astype(F32)).astype(BF16)
            start(near_copy(r, 1, 1))
        grams = grams_of(x)
        own_block[1, 0:256, :] = grams[1]
        own_block[1, 256:320, :] = crosses_of(1, x)
        start(remote(own_block.at[1], own_block.at[0], own_send, own_recv, device(1)))
        own_block[0, 0:256, :] = grams[0]
        own_block[0, 256:320, :] = crosses_of(0, x)

        finish_sums()
        for i in range(3):
            remote(end_beta, end_beta if i == 2 else end_part.at[i], end_send.at[i], end_recv.at[i],
                   device(1)).wait_recv()
        product = end_part[0] + end_part[1]
        coef_out[...] = soften(end_beta[...] - step * (product - cross_state[0]), threshold)
        for copy in sent:
            copy.wait_send()


def copy_out(gram, cross, coef, gram_out, cross_out, coef_out, gram_here, cross_here, coef_here, sems_in, sems_out):
    stages = ((gram, gram_here, gram_out), (cross, cross_here, cross_out), (coef, coef_here, coef_out))
    ins = [pltpu.make_async_copy(source, here, sems_in.at[i]) for i, (source, here, _) in enumerate(stages)]
    outs = [pltpu.make_async_copy(here, out, sems_out.at[i]) for i, (_, here, out) in enumerate(stages)]
    for copy in ins:
        copy.start()
    for arrived, copy in zip(ins, outs):
        arrived.wait()
        copy.start()
    for copy in outs:
        copy.wait()


def body(expr_stretch, target_stretch, subsample, gram_state, cross_state, step_size, penalty):
    vmem = pl.BlockSpec(memory_space=pltpu.VMEM)
    hbm = pl.BlockSpec(memory_space=pltpu.HBM)
    dma = pltpu.SemaphoreType.DMA
    out_shape = (
        jax.ShapeDtypeStruct((256, 256), F32),
        jax.ShapeDtypeStruct((64, 256), F32),
        jax.ShapeDtypeStruct((64, 256), F32),
    )
    results = pl.pallas_call(
        kernel,
        out_shape=out_shape,
        in_specs=[hbm] * 7,
        out_specs=(vmem, vmem, vmem),
        scratch_shapes=[
            pltpu.VMEM((64, 384), BF16),
            pltpu.VMEM((2, CELLS), jnp.int32),
            pltpu.VMEM((2, 256, 256), F32),
            pltpu.VMEM((2, 64, 256), F32),
            pltpu.SMEM((2,), F32),
            pltpu.SMEM((2,), F32),
            pltpu.VMEM((2, RING, 256, 256), BF16),
            pltpu.VMEM((2, 2, RING, 128, 256), BF16),
            pltpu.VMEM((2, 64, 256), F32),
            pltpu.VMEM((2, 2, 64, 256), BF16),
            pltpu.VMEM((2, 2, 128, 256), F32),
            pltpu.VMEM((2, 2, 64, 256), F32),
            pltpu.VMEM((64, 256), BF16),
            pltpu.VMEM((RING, 96, 128), BF16),
            pltpu.VMEM((2, RING, 96, 512), BF16),
            pltpu.VMEM((RING, 2, 96, 128), BF16),
            pltpu.VMEM((RING, 768, 128), BF16),
            pltpu.VMEM((2, 2, 512, 768), BF16),
            pltpu.VMEM((384, 128), BF16),
            pltpu.VMEM((192, 128), BF16),
            pltpu.VMEM((192, 128), BF16),
            pltpu.VMEM((2, 2, 128, 256), F32),
            pltpu.VMEM((2, 2, 768), F32),
            pltpu.VMEM((256, 256), BF16),
            pltpu.VMEM((2, 3, 320, 256), BF16),
            pltpu.VMEM((2, 320, 256), BF16),
            pltpu.VMEM((2, 320, 256), F32),
            pltpu.VMEM((2, 320, 256), BF16),
            pltpu.VMEM((2, 64, 256), F32),
            pltpu.VMEM((64, 256), F32),
            pltpu.VMEM((64, 256), F32),
            dma((6, 2, 4)), dma((6, 2, 4)),
            dma((7,)), dma((7,)),
            dma((2, 2, 2)), dma((2, 2, 2)),
            dma((2, 2)), dma((2, 2)),
            dma((2, 2)), dma((2, 2)),
            dma((2, 2, 2)), dma((2, 2)),
            dma((2,)), dma((2,)),
            dma((3,)), dma((3,)),
            dma, dma,
            dma, dma,
            dma((3,)),
            dma((6,)),
            dma((RING,)),
            dma((4,)),
            dma((2, 7)), dma((2, 7)),
        ],
        compiler_params=pltpu.CompilerParams(
            collective_id=0, has_side_effects=True, vmem_limit_bytes=60 * 2**20),
    )(
        expr_stretch,
        target_stretch.T,
        subsample,
        gram_state[:, 0],
        jnp.swapaxes(cross_state[:, 0], 1, 2),
        step_size,
        penalty,
    )
    gram, cross, coef = pl.pallas_call(
        copy_out,
        out_shape=out_shape,
        in_specs=[hbm] * 3,
        out_specs=(hbm, hbm, hbm),
        scratch_shapes=[
            pltpu.VMEM((256, 256), F32),
            pltpu.VMEM((64, 256), F32),
            pltpu.VMEM((64, 256), F32),
            dma((3,)),
            dma((3,)),
        ],
        compiler_params=pltpu.CompilerParams(vmem_limit_bytes=60 * 2**20),
    )(*results)
    return gram[None], cross.T[None], coef.T[None]


def solution(mesh):
    return jax.shard_map(
        body,
        mesh=mesh,
        in_specs=(
            P("reg", None),
            P("reg", "tgt"),
            P(),
            P(None, "grp", "reg", "tgt"),
            P(None, "grp", "reg", "tgt"),
            P(),
            P(),
        ),
        out_specs=(P("grp", "reg", "tgt"), P("grp", "reg", "tgt"), P("grp", "reg", "tgt")),
        check_vma=False,
    )
```

```python
import jax
import jax.numpy as jnp
from jax import lax
from jax.experimental import pallas as pl
from jax.experimental.pallas import tpu as pltpu
from jax.sharding import PartitionSpec as P

RING = 8
CELLS = 6144
F32, BF16 = jnp.float32, jnp.bfloat16
ROWS_T = (((1,), (1,)), ((), ()))


def soften(values, threshold):
    return values - jnp.clip(values, -threshold, threshold)


def kernel(
    expr, target_hbm, subsample_hbm, gram_hbm, cross_hbm, step_hbm, penalty_hbm,
    gram_out, cross_out, coef_out,
    target, subsample, gram_state, cross_state, step_size, penalty,
    gbuf, bbuf, cross_fit, bsend, acc, precv,
    bsend_zero, stage, cbuf, tbuf, rbuf, lhs, tpad, tsend, trecv, crosses, wbuf, gsend,
    blocks, xsend, xpass, own_block, xrecv, end_part, end_beta, beta_keep,
    ring_send, ring_recv, spread_send, spread_recv, piece_send, piece_recv,
    part_send, part_recv, far_send, far_recv, near_send, near_recv,
    feed_send, feed_recv, end_send, end_recv, own_send, own_recv,
    swap_send, swap_recv, local_sem, load_sem, stage_sem, first_send, reach_send, reach_recv,
):
    c = lax.axis_index("grp")
    reg = lax.axis_index("reg")
    tgt = lax.axis_index("tgt")
    z, xh = reg // 2, reg % 2
    y, xl = tgt // 2, tgt % 2
    x = xh * 2 + xl

    def device(core, zz=z, hi=xh, yy=y, lo=xl):
        return (core, zz * 2 + hi, yy * 2 + lo)

    def chip_x(index, core):
        return device(core, hi=index // 2, lo=index % 2)

    def remote(src, dst, send, recv, to):
        return pltpu.make_async_remote_copy(
            src_ref=src, dst_ref=dst, send_sem=send, recv_sem=recv,
            device_id=to, device_id_type=pl.DeviceIdType.MESH,
        )

    right, left = (x + 1) % 4, (x + 3) % 4
    barrier = pltpu.get_barrier_semaphore()

    def greet(peers):
        for peer in peers:
            pl.semaphore_signal(barrier, inc=1, device_id=peer, device_id_type=pl.DeviceIdType.MESH)

    def load(index, source, here):
        copy = pltpu.make_async_copy(source, here, load_sem.at[index])
        copy.start()
        return copy

    def rings(core, view_of, along_y):
        def ring_copy(ring, part, way, hop, chunk):
            here = y if ring in along_y else z
            there = (here + (1 if way == 0 else RING - 1)) % RING
            view = view_of(ring, part, chunk)
            slot = ring * 2 + part
            return remote(view, view, ring_send.at[slot, way, hop - 1], ring_recv.at[slot, way, hop - 1],
                          device(core, yy=there) if ring in along_y else device(core, zz=there))

        def ring_start(ring, part):
            here = y if ring in along_y else z
            for way in range(2):
                ring_copy(ring, part, way, 1, here).start()

        def arrived(ring, way, hop):
            here = y if ring in along_y else z
            return (here + (RING - hop if way == 0 else hop)) % RING

        def ring_step(ring, part, hop):
            for way in range(2):
                chunk = arrived(ring, way, hop)
                ring_copy(ring, part, way, hop, chunk).wait_recv()
                if way == part:
                    ring_copy(ring, part, way, hop + 1, chunk).start()
                else:
                    @pl.when(hop < 3)
                    def _():
                        ring_copy(ring, part, way, hop + 1, chunk).start()

        def ring_last(ring, part):
            ring_copy(ring, part, part, 4, arrived(ring, part, 4)).wait_recv()

        def ring_drain(ring, part, first=1):
            @pl.loop(first, 5)
            def _(hop):
                for way in range(2):
                    copy = ring_copy(ring, part, way, hop, arrived(ring, way, hop - 1))
                    if way == part:
                        copy.wait_send()
                    else:
                        pl.when(hop < 4)(copy.wait_send)

        return ring_start, ring_step, ring_last, ring_drain

    def finish_sums():
        for way in range(2):
            for half in range(2):
                rows = pl.ds(160 * half, 160)
                remote(xsend.at[0, 1 + way, rows], xrecv.at[way, rows], near_send.at[0, way, half],
                       near_recv.at[way, half], chip_x(left if way else right, 0)).wait_recv()
        sums = own_block[0] + xrecv[0].astype(F32) + xrecv[1].astype(F32)
        gram_out[...] = gram_state[1] + sums[0:256] / CELLS
        cross_out[...] = cross_state[1] + sums[256:320] / CELLS

    @pl.when(c == 1)
    def _():
        GRAM, BETA = 0, 1
        loads = [
            load(0, step_hbm, step_size), load(1, penalty_hbm, penalty),
            load(2, cross_hbm, cross_state), load(3, gram_hbm, gram_state),
        ]
        peers = [device(1, zz=(z + d) % RING) for d in (1, 2, 6, 7)]
        peers += [device(core, yy=(y + d) % RING) for core in (0, 1) for d in (1, 7)]
        peers += [chip_x((x + d) % 4, core) for core in (0, 1) for d in (1, 2, 3)]
        peers += [device(0)]
        greet(peers)
        sent = []

        def start(copy):
            copy.start()
            sent.append(copy)

        def view_of(ring, part, chunk):
            if ring == GRAM:
                return gbuf.at[part, chunk]
            return bbuf.at[ring - BETA, part, chunk]

        ring_start, ring_step, ring_last, ring_drain = rings(1, view_of, (GRAM,))
        own_k = xl == xh

        def own_half(ref_index):
            return pl.ds(pl.multiple_of(ref_index * 64, 64), 64)

        def piece_slot(it, r, lo):
            return bbuf.at[it, r, z, own_half(lo)]

        def piece_near(it, r):
            return remote(bsend.at[it, r], piece_slot(it, r, xl), piece_send.at[it, r, 1],
                          piece_recv.at[it, r, xl], device(1, lo=1 - xl))

        def pieces_start(it, r):
            start(remote(bsend.at[it, r], piece_slot(it, r, xl), piece_send.at[it, r, 0],
                         piece_recv.at[it, r, xl], device(1, hi=1 - xh, lo=xh)))

            @pl.when(own_k)
            def _():
                pltpu.make_async_copy(
                    bsend.at[it, r], piece_slot(it, r, xl), piece_recv.at[it, r, xl]).start()

            @pl.when(jnp.logical_not(own_k))
            def _():
                piece_near(it, r).start()

        def pieces_wait(it, r):
            for lo in range(2):
                pltpu.make_async_copy(
                    bsend.at[it, r], piece_slot(it, r, lo), piece_recv.at[it, r, lo]).wait()

        def product_of(it, r, distance):
            k = ((y if it == 0 else z) + distance) % RING
            return lax.dot_general(bbuf[it, r, k], gbuf[r, k], ROWS_T, preferred_element_type=F32)

        def first_products(it, r, start_at, count):
            acc[it, r] = jnp.zeros((128, 256), F32)

            @pl.loop(0, count)
            def _(j):
                acc[it, r] += product_of(it, r, start_at + j)

        def add_products(it, r, distances):
            total = acc[it, r]
            for distance in distances:
                total = total + product_of(it, r, distance)
            acc[it, r] = total

        def part_copy(it, r):
            return remote(acc.at[it, r, own_half(1 - xl)], precv.at[it, r],
                          part_send.at[it, r], part_recv.at[it, r], device(1, lo=1 - xl))

        def step_of(r):
            return step_size[r], step_size[r] * penalty[r]

        def next_beta(it, r, beta):
            step, threshold = step_of(r)
            part_copy(it, r).wait_recv()
            product = acc[it, r, own_half(xl)] + precv[it, r]
            return soften(beta - step * (product - cross_fit[r]), threshold)

        for copy in loads:
            copy.wait()
        gbuf[1, y] = gram_state[0].astype(BF16)
        cross_fit[1] = cross_state[0]
        step, threshold = step_of(1)
        beta_one = soften(step * cross_state[0], threshold)
        bsend[0, 1] = beta_one.astype(BF16)
        pl.semaphore_wait(barrier, len(peers))

        ring_start(GRAM, 1)
        pieces_start(0, 1)
        cross_feed = remote(cross_state.at[0], cross_fit.at[0], feed_send.at[1], feed_recv.at[1], device(0))
        gram_feed = remote(gsend, gbuf.at[0, y], feed_send.at[0], feed_recv.at[0], device(0))
        for r in (1, 0):
            pieces_wait(0, r)
            ring_start(BETA, r)

        @pl.loop(1, 4)
        def _(hop):
            for r in (1, 0):
                ring_step(GRAM, r, hop)
            for r in (1, 0):
                ring_step(BETA, r, hop)

        for r in (1, 0):
            ring_last(BETA, r)
        cross_feed.wait_recv()
        step, threshold = step_of(0)
        beta_zero = soften(step * cross_fit[0], threshold)
        gram_feed.wait_recv()
        for r in (1, 0):
            first_products(0, r, 5, 7)
        for r in (1, 0):
            ring_last(GRAM, r)
            add_products(0, r, (4,))
            start(part_copy(0, r))
        betas = [beta_zero, beta_one]
        for r in (1, 0):
            betas[r] = next_beta(0, r, betas[r])
            bsend[1, r] = betas[r].astype(BF16)
            pieces_start(1, r)
        beta_keep[...] = betas[0]
        start(remote(beta_keep, end_beta, end_send.at[2], end_recv.at[2], device(0)))
        def reach_copy(r, slot, chunk, to):
            view = bbuf.at[1, r, chunk % RING]
            return remote(view, view, reach_send.at[r, slot], reach_recv.at[r, slot],
                          device(1, zz=(z + to) % RING))

        M1, P1, M2, P2, M3, P3, FAR = range(7)
        for r in (1, 0):
            pieces_wait(1, r)
            start(reach_copy(r, M2, z, 2))
            start(reach_copy(r, P2, z, 6))
            start(reach_copy(r, M1, z, 1))
            start(reach_copy(r, P1, z, 7))
        for r in (1, 0):
            reach_copy(r, M2, z + 6, 2).wait_recv()
            start(reach_copy(r, M3, z + 6, 1))
            if r == 0:
                start(reach_copy(r, FAR, z + 6, 2))
            reach_copy(r, P2, z + 2, 6).wait_recv()
            start(reach_copy(r, P3, z + 2, 7))
            if r == 1:
                start(reach_copy(r, FAR, z + 2, 6))
        for r in (1, 0):
            reach_copy(r, M1, z + 7, 1).wait_recv()
            reach_copy(r, P1, z + 1, 7).wait_recv()
            first_products(1, r, 6, 5)

        def last_products(r):
            reach_copy(r, M3, z + 5, 1).wait_recv()
            reach_copy(r, P3, z + 3, 7).wait_recv()
            reach_copy(r, FAR, z + 4, 2).wait_recv()
            add_products(1, r, (3, 4, 5))

        last_products(1)
        start(part_copy(1, 1))
        last_products(0)
        start(remote(acc.at[1, 0, own_half(1 - xl)], end_part.at[1], end_send.at[1], end_recv.at[1],
                     device(0, lo=1 - xl)))
        start(remote(acc.at[1, 0, own_half(xl)], end_part.at[0], end_send.at[0], end_recv.at[0], device(0)))
        remote(own_block.at[1], own_block.at[0], own_send, own_recv, device(0)).wait_recv()
        finish_sums()
        coef_out[...] = next_beta(1, 1, betas[1])

        for copy in sent:
            copy.wait_send()
        ring_drain(GRAM, 1)
        ring_drain(GRAM, 0, 2)
        for r in range(2):
            ring_drain(BETA, r)
        for it, r in ((0, 1), (1, 0), (1, 1)):
            @pl.when(jnp.logical_not(own_k))
            def _():
                piece_near(it, r).wait_send()

    @pl.when(c == 0)
    def _():
        COLS, ROWS, TARGETS = 0, 1, 2
        row0 = pl.multiple_of(xl * 192, 16)
        row0_other = pl.multiple_of((1 - xl) * 192, 16)
        part_h, part_q = y // 4, y % 4
        rows_h = pl.multiple_of(xl * 192 + part_h * 96, 16)

        def at96(index):
            return pl.ds(pl.multiple_of(index * 96, 16), 96)

        def expr_cols(index):
            return pl.ds(pl.multiple_of(index * 512 + part_q * 128, 128), 128)

        peers = [device(0, zz=(z + d) % RING) for d in range(1, RING)]
        peers += [device(core, yy=(y + d) % RING) for core in (0, 1) for d in (1, 7)]
        peers += [chip_x(right, 0), chip_x(left, 0), device(1)]
        peers += [chip_x((x + d) % 4, 1) for d in (1, 2, 3)]
        greet(peers)
        loads = [
            load(0, step_hbm, step_size), load(1, penalty_hbm, penalty), load(2, cross_hbm, cross_state),
            load(3, gram_hbm, gram_state),
        ]
        def stage_copy(d):
            return pltpu.make_async_copy(
                expr.at[pl.ds(rows_h, 96), expr_cols((z + d) % RING)], stage.at[d], stage_sem.at[d])

        def spread_copy(d, to, source):
            return remote(stage.at[d], rbuf.at[y, at96(source)], spread_send.at[d - 1], spread_recv.at[d - 1],
                          device(0, zz=to))

        @pl.loop(1, RING)
        def _(d):
            stage_copy(d).start()

        local = [
            pltpu.make_async_copy(
                expr.at[pl.ds(pl.multiple_of(row0 + h * 96, 16), 96), pl.ds(pl.multiple_of(y * 512, 512), 512)],
                cbuf.at[h, z], local_sem.at[h])
            for h in range(2)
        ]
        local.append(pltpu.make_async_copy(
            expr.at[pl.ds(rows_h, 96), expr_cols(z)], rbuf.at[y, at96(z)], local_sem.at[2]))
        for copy in local:
            copy.start()
        loads += [load(4, target_hbm, target), load(5, subsample_hbm, subsample)]
        sent = []

        def start(copy):
            copy.start()
            sent.append(copy)

        def view_of(ring, part, chunk):
            if ring == COLS:
                return cbuf.at[part, chunk]
            if ring == TARGETS:
                return tbuf.at[chunk]
            return rbuf.at[chunk, pl.ds(part * 384, 384)]

        ring_start, ring_step, ring_last, ring_drain = rings(0, view_of, (ROWS,))

        for copy in loads[:4]:
            copy.wait()
        gsend[...] = gram_state[0].astype(BF16)
        step = step_size[0]
        threshold = step * penalty[0]
        bsend_zero[...] = soften(step * cross_state[0], threshold).astype(BF16)
        pl.semaphore_wait(barrier, len(peers))

        for way in range(2):
            start(remote(gsend, gbuf.at[0, y], first_send.at[way], ring_recv.at[0, way, 0],
                         device(1, yy=(y + (7 if way else 1)) % RING)))
        for i, hi in enumerate((1 - xh, xh)):
            start(remote(bsend_zero, bbuf.at[0, 0, z, pl.ds(pl.multiple_of(xl * 64, 64), 64)], first_send.at[2 + i],
                         piece_recv.at[0, 0, xl], device(1, hi=hi, lo=xh)))
        @pl.loop(1, RING)
        def _(d):
            stage_copy(d).wait()
            spread_copy(d, (z + d) % RING, z).start()

        for copy in local:
            copy.wait()
        for part in range(2):
            ring_start(COLS, part)
        start(remote(gsend, gbuf.at[0, y], feed_send.at[0], feed_recv.at[0], device(1)))
        start(remote(cross_state.at[0], cross_fit.at[0], feed_send.at[1], feed_recv.at[1], device(1)))
        loads[4].wait()
        both = jnp.concatenate([target[...], target[...]], axis=0)
        lane_half = lax.broadcasted_iota(jnp.int32, both.shape, 0) // 64
        both = jnp.where(lane_half == xl, both, jnp.zeros_like(both))
        tpad[...] = both.T
        tsend[...] = tpad[pl.ds(row0_other, 192), :]
        swap = remote(tsend, trecv, swap_send, swap_recv, device(0, lo=1 - xl))
        start(swap)
        @pl.loop(1, RING)
        def _(d):
            spread_copy(d, z, (z + RING - d) % RING).wait_recv()

        for part in range(2):
            ring_start(ROWS, part)
        swap.wait_recv()
        for h in range(2):
            tbuf[z, h] = (
                tpad[pl.ds(pl.multiple_of(row0 + h * 96, 16), 96), :] + trecv[h * 96:(h + 1) * 96, :])
        ring_start(TARGETS, 0)

        loads[5].wait()
        first_lane = xh * 384 + xl * 192
        lane = lax.broadcasted_iota(jnp.int32, (2, 768), 1)
        for h in range(2):
            weights = jnp.zeros((2, 768), F32)
            for zz in range(RING):
                cells = subsample[:, zz * 768:(zz + 1) * 768].astype(F32)
                moved = pltpu.roll(cells, (1536 + zz * 96 - h * 96 - first_lane) % 768, axis=1)
                weights = jnp.where((lane >= zz * 96) & (lane < zz * 96 + 96), moved, weights)
            wbuf[h] = weights

        def weigh(distance):
            chunk = (y + distance) % RING
            h, q = chunk // 4, chunk % 4
            block = rbuf[chunk].T
            rows = pl.ds(pl.multiple_of(q * 128, 128), 128)
            pair = wbuf[h].astype(BF16)
            for r in range(2):
                lhs[r, h, rows, :] = block * pair[r:r + 1, :]

        @pl.loop(1, 4)
        def _(hop):
            for part in range(2):
                ring_step(ROWS, part, hop)
            for part in range(2):
                ring_step(COLS, part, hop)
            ring_step(TARGETS, 0, hop)

            @pl.loop(0, 2)
            def _(way):
                weigh((hop - 1) * (1 + 6 * way) % RING)

        for part in range(2):
            ring_last(COLS, part)
        ring_last(TARGETS, 0)

        @pl.loop(0, 2)
        def _(way):
            weigh(3 + 2 * way)

        for part in range(2):
            ring_last(ROWS, part)
        weigh(4)

        def rows_of(hi, h):
            half = pl.ds(pl.multiple_of(hi * 256, 256), 256)
            return jnp.concatenate([lhs[0, h, half, :], lhs[1, h, half, :]], axis=0)

        @pl.loop(0, 2)
        def _(hi):
            total = jnp.zeros((512, 128), F32)
            for h in range(2):
                total += jnp.dot(rows_of(hi, h), tbuf[:, h].reshape(768, 128), preferred_element_type=F32)
            for r in range(2):
                crosses[hi, r] = total[r * 256:(r + 1) * 256].T

        def crosses_of(r, index):
            return crosses[index // 2, r, pl.ds(pl.multiple_of((index % 2) * 64, 64), 64), :]

        top, low = pl.ds(0, 160), pl.ds(160, 160)

        def far_copy(r, half):
            rows = low if half else top
            return remote(xsend.at[r, 0, rows], xpass.at[r, rows], far_send.at[r, half], far_recv.at[r, half],
                          chip_x(left if half else right, 0))

        def near_copy(r, way, half):
            rows = low if half else top
            return remote(xsend.at[r, 1 + way, rows], xrecv.at[way, rows], near_send.at[r, way, half],
                          near_recv.at[way, half], chip_x(left if way else right, r))

        far = (x + 2) % 4

        @pl.loop(0, 4)
        def _(k):
            index = (x + 2 + 3 * k + 3 * (k // 2) + 2 * (k // 3)) % 4
            hi, lo = index // 2, index % 2
            total = jnp.zeros((512, 256), F32)
            for h in range(2):
                cols = cbuf[h, :, :, pl.ds(pl.multiple_of(lo * 256, 256), 256)].reshape(768, 256)
                total += jnp.dot(rows_of(hi, h), cols, preferred_element_type=F32)
            blocks[k] = total

            @pl.when(k == 0)
            def _():
                for r in (1, 0):
                    xsend[r, 0, 0:256, :] = blocks[0, r * 256:(r + 1) * 256].astype(BF16)
                    xsend[r, 0, 256:320, :] = crosses_of(r, far).astype(BF16)
                    far_copy(r, 0).start()
                    far_copy(r, 1).start()

            @pl.when(k == 1)
            def _():
                for r in (1, 0):
                    xsend[r, 1, 160:256, :] = blocks[1, r * 256 + 160:(r + 1) * 256].astype(BF16)
                    xsend[r, 1, 256:320, :] = crosses_of(r, right).astype(BF16)
                    near_copy(r, 0, 1).start()

            @pl.when(k == 2)
            def _():
                for r in (1, 0):
                    xsend[r, 2, 0:160, :] = blocks[2, r * 256:r * 256 + 160].astype(BF16)
                    near_copy(r, 1, 0).start()

        for r in (1, 0):
            far_copy(r, 0).wait_recv()
            xsend[r, 1, 0:160, :] = (
                blocks[1, r * 256:r * 256 + 160] + xpass[r, 0:160, :].astype(F32)).astype(BF16)
            near_copy(r, 0, 0).start()
            far_copy(r, 1).wait_recv()
            xsend[r, 2, 160:256, :] = (
                blocks[2, r * 256 + 160:(r + 1) * 256] + xpass[r, 160:256, :].astype(F32)).astype(BF16)
            xsend[r, 2, 256:320, :] = (crosses_of(r, left) + xpass[r, 256:320, :].astype(F32)).astype(BF16)
            near_copy(r, 1, 1).start()
        for r in (1, 0):
            own_block[r, 0:256, :] = blocks[3, r * 256:(r + 1) * 256]
            own_block[r, 256:320, :] = crosses_of(r, x)
        start(remote(own_block.at[1], own_block.at[0], own_send, own_recv, device(1)))

        finish_sums()
        for i in range(3):
            remote(end_beta, end_beta if i == 2 else end_part.at[i], end_send.at[i], end_recv.at[i],
                   device(1)).wait_recv()
        product = end_part[0] + end_part[1]
        coef_out[...] = soften(end_beta[...] - step * (product - cross_state[0]), threshold)
        for copy in sent:
            copy.wait_send()
        for part in range(2):
            ring_drain(COLS, part)
            ring_drain(ROWS, part)
        ring_drain(TARGETS, 0)

        @pl.loop(1, RING)
        def _(d):
            spread_copy(d, (z + d) % RING, z).wait_send()

        for r in range(2):
            for half in range(2):
                far_copy(r, half).wait_send()
                for way in range(2):
                    near_copy(r, way, half).wait_send()


def copy_out(gram, cross, coef, gram_out, cross_out, coef_out, gram_here, cross_here, coef_here, sems_in, sems_out):
    stages = ((gram, gram_here, gram_out), (cross, cross_here, cross_out), (coef, coef_here, coef_out))
    ins = [pltpu.make_async_copy(source, here, sems_in.at[i]) for i, (source, here, _) in enumerate(stages)]
    outs = [pltpu.make_async_copy(here, out, sems_out.at[i]) for i, (_, here, out) in enumerate(stages)]
    for copy in ins:
        copy.start()
    for arrived, copy in zip(ins, outs):
        arrived.wait()
        copy.start()
    for copy in outs:
        copy.wait()


def body(expr_stretch, target_stretch, subsample, gram_state, cross_state, step_size, penalty):
    vmem = pl.BlockSpec(memory_space=pltpu.VMEM)
    hbm = pl.BlockSpec(memory_space=pltpu.HBM)
    dma = pltpu.SemaphoreType.DMA
    out_shape = (
        jax.ShapeDtypeStruct((256, 256), F32),
        jax.ShapeDtypeStruct((64, 256), F32),
        jax.ShapeDtypeStruct((64, 256), F32),
    )
    results = pl.pallas_call(
        kernel,
        out_shape=out_shape,
        in_specs=[hbm] * 7,
        out_specs=(vmem, vmem, vmem),
        scratch_shapes=[
            pltpu.VMEM((64, 384), BF16),
            pltpu.VMEM((2, CELLS), jnp.int32),
            pltpu.VMEM((2, 256, 256), F32),
            pltpu.VMEM((2, 64, 256), F32),
            pltpu.SMEM((2,), F32),
            pltpu.SMEM((2,), F32),
            pltpu.VMEM((2, RING, 256, 256), BF16),
            pltpu.VMEM((2, 2, RING, 128, 256), BF16),
            pltpu.VMEM((2, 64, 256), F32),
            pltpu.VMEM((2, 2, 64, 256), BF16),
            pltpu.VMEM((2, 2, 128, 256), F32),
            pltpu.VMEM((2, 2, 64, 256), F32),
            pltpu.VMEM((64, 256), BF16),
            pltpu.VMEM((RING, 96, 128), BF16),
            pltpu.VMEM((2, RING, 96, 512), BF16),
            pltpu.VMEM((RING, 2, 96, 128), BF16),
            pltpu.VMEM((RING, 768, 128), BF16),
            pltpu.VMEM((2, 2, 512, 768), BF16),
            pltpu.VMEM((384, 128), BF16),
            pltpu.VMEM((192, 128), BF16),
            pltpu.VMEM((192, 128), BF16),
            pltpu.VMEM((2, 2, 128, 256), F32),
            pltpu.VMEM((2, 2, 768), F32),
            pltpu.VMEM((256, 256), BF16),
            pltpu.VMEM((4, 512, 256), F32),
            pltpu.VMEM((2, 3, 320, 256), BF16),
            pltpu.VMEM((2, 320, 256), BF16),
            pltpu.VMEM((2, 320, 256), F32),
            pltpu.VMEM((2, 320, 256), BF16),
            pltpu.VMEM((2, 64, 256), F32),
            pltpu.VMEM((64, 256), F32),
            pltpu.VMEM((64, 256), F32),
            dma((6, 2, 4)), dma((6, 2, 4)),
            dma((7,)), dma((7,)),
            dma((2, 2, 2)), dma((2, 2, 2)),
            dma((2, 2)), dma((2, 2)),
            dma((2, 2)), dma((2, 2)),
            dma((2, 2, 2)), dma((2, 2)),
            dma((2,)), dma((2,)),
            dma((3,)), dma((3,)),
            dma, dma,
            dma, dma,
            dma((3,)),
            dma((6,)),
            dma((RING,)),
            dma((4,)),
            dma((2, 7)), dma((2, 7)),
        ],
        compiler_params=pltpu.CompilerParams(
            collective_id=0, has_side_effects=True, vmem_limit_bytes=60 * 2**20),
    )(
        expr_stretch,
        target_stretch.T,
        subsample,
        gram_state[:, 0],
        jnp.swapaxes(cross_state[:, 0], 1, 2),
        step_size,
        penalty,
    )
    gram, cross, coef = pl.pallas_call(
        copy_out,
        out_shape=out_shape,
        in_specs=[hbm] * 3,
        out_specs=(hbm, hbm, hbm),
        scratch_shapes=[
            pltpu.VMEM((256, 256), F32),
            pltpu.VMEM((64, 256), F32),
            pltpu.VMEM((64, 256), F32),
            dma((3,)),
            dma((3,)),
        ],
        compiler_params=pltpu.CompilerParams(vmem_limit_bytes=60 * 2**20),
    )(*results)
    return gram[None], cross.T[None], coef.T[None]


def solution(mesh):
    return jax.shard_map(
        body,
        mesh=mesh,
        in_specs=(
            P("reg", None),
            P("reg", "tgt"),
            P(),
            P(None, "grp", "reg", "tgt"),
            P(None, "grp", "reg", "tgt"),
            P(),
            P(),
        ),
        out_specs=(P("grp", "reg", "tgt"), P("grp", "reg", "tgt"), P("grp", "reg", "tgt")),
        check_vma=False,
    )
```

```python
import jax
import jax.numpy as jnp
from jax import lax
from jax.experimental import pallas as pl
from jax.experimental.pallas import tpu as pltpu
from jax.sharding import PartitionSpec as P

RING = 8
CELLS = 6144
F32, BF16 = jnp.float32, jnp.bfloat16
ROWS_T = (((1,), (1,)), ((), ()))


def soften(values, threshold):
    return values - jnp.clip(values, -threshold, threshold)


def kernel(
    expr, target_hbm, subsample_hbm, gram_hbm, cross_hbm, step_hbm, penalty_hbm,
    gram_out, cross_out, coef_out,
    target, subsample, gram_state, cross_state, step_size, penalty,
    gbuf, bbuf, cross_fit, bsend, acc, precv,
    bsend_zero, stage, cbuf, tbuf, rbuf, lhs, tpad, tsend, trecv, crosses, wbuf, gsend,
    blocks, xsend, xpass, own_block, xrecv, end_part, end_beta, beta_keep,
    ring_send, ring_recv, spread_send, spread_recv, piece_send, piece_recv,
    part_send, part_recv, far_send, far_recv, near_send, near_recv,
    feed_send, feed_recv, end_send, end_recv, own_send, own_recv,
    swap_send, swap_recv, local_sem, load_sem, stage_sem, first_send, reach_send, reach_recv,
):
    c = lax.axis_index("grp")
    reg = lax.axis_index("reg")
    tgt = lax.axis_index("tgt")
    z, xh = reg // 2, reg % 2
    y, xl = tgt // 2, tgt % 2
    x = xh * 2 + xl

    def device(core, zz=z, hi=xh, yy=y, lo=xl):
        return (core, zz * 2 + hi, yy * 2 + lo)

    def chip_x(index, core):
        return device(core, hi=index // 2, lo=index % 2)

    def remote(src, dst, send, recv, to):
        return pltpu.make_async_remote_copy(
            src_ref=src, dst_ref=dst, send_sem=send, recv_sem=recv,
            device_id=to, device_id_type=pl.DeviceIdType.MESH,
        )

    right, left = (x + 1) % 4, (x + 3) % 4
    barrier = pltpu.get_barrier_semaphore()

    def greet(peers):
        for peer in peers:
            pl.semaphore_signal(barrier, inc=1, device_id=peer, device_id_type=pl.DeviceIdType.MESH)

    def load(index, source, here):
        copy = pltpu.make_async_copy(source, here, load_sem.at[index])
        copy.start()
        return copy

    def rings(core, view_of, along_y):
        def ring_copy(ring, part, way, hop, chunk):
            here = y if ring in along_y else z
            there = (here + (1 if way == 0 else RING - 1)) % RING
            view = view_of(ring, part, chunk)
            slot = ring * 2 + part
            return remote(view, view, ring_send.at[slot, way, hop - 1], ring_recv.at[slot, way, hop - 1],
                          device(core, yy=there) if ring in along_y else device(core, zz=there))

        def ring_start(ring, part):
            here = y if ring in along_y else z
            for way in range(2):
                ring_copy(ring, part, way, 1, here).start()

        def arrived(ring, way, hop):
            here = y if ring in along_y else z
            return (here + (RING - hop if way == 0 else hop)) % RING

        def ring_step(ring, part, hop):
            for way in range(2):
                chunk = arrived(ring, way, hop)
                ring_copy(ring, part, way, hop, chunk).wait_recv()
                if way == part:
                    ring_copy(ring, part, way, hop + 1, chunk).start()
                else:
                    @pl.when(hop < 3)
                    def _():
                        ring_copy(ring, part, way, hop + 1, chunk).start()

        def ring_last(ring, part):
            ring_copy(ring, part, part, 4, arrived(ring, part, 4)).wait_recv()

        def ring_drain(ring, part, first=1):
            @pl.loop(first, 5)
            def _(hop):
                for way in range(2):
                    copy = ring_copy(ring, part, way, hop, arrived(ring, way, hop - 1))
                    if way == part:
                        copy.wait_send()
                    else:
                        pl.when(hop < 4)(copy.wait_send)

        return ring_start, ring_step, ring_last, ring_drain

    def finish_sums():
        for way in range(2):
            for half in range(2):
                rows = pl.ds(160 * half, 160)
                remote(xsend.at[0, 1 + way, rows], xrecv.at[way, rows], near_send.at[0, way, half],
                       near_recv.at[way, half], chip_x(left if way else right, 0)).wait_recv()
        sums = own_block[0] + xrecv[0].astype(F32) + xrecv[1].astype(F32)
        gram_out[...] = gram_state[1] + sums[0:256] / CELLS
        cross_out[...] = cross_state[1] + sums[256:320] / CELLS

    @pl.when(c == 1)
    def _():
        GRAM, BETA = 0, 1
        loads = [
            load(0, step_hbm, step_size), load(1, penalty_hbm, penalty),
            load(2, cross_hbm, cross_state), load(3, gram_hbm, gram_state),
        ]
        peers = [device(1, zz=(z + d) % RING) for d in (1, 2, 6, 7)]
        peers += [device(core, yy=(y + d) % RING) for core in (0, 1) for d in (1, 7)]
        peers += [chip_x((x + d) % 4, core) for core in (0, 1) for d in (1, 2, 3)]
        peers += [device(0)]
        greet(peers)
        sent = []

        def start(copy):
            copy.start()
            sent.append(copy)

        def view_of(ring, part, chunk):
            if ring == GRAM:
                return gbuf.at[part, chunk]
            return bbuf.at[ring - BETA, part, chunk]

        ring_start, ring_step, ring_last, ring_drain = rings(1, view_of, (GRAM,))
        own_k = xl == xh

        def own_half(ref_index):
            return pl.ds(pl.multiple_of(ref_index * 64, 64), 64)

        def piece_slot(it, r, lo):
            return bbuf.at[it, r, z, own_half(lo)]

        def piece_near(it, r):
            return remote(bsend.at[it, r], piece_slot(it, r, xl), piece_send.at[it, r, 1],
                          piece_recv.at[it, r, xl], device(1, lo=1 - xl))

        def pieces_start(it, r):
            start(remote(bsend.at[it, r], piece_slot(it, r, xl), piece_send.at[it, r, 0],
                         piece_recv.at[it, r, xl], device(1, hi=1 - xh, lo=xh)))

            @pl.when(own_k)
            def _():
                pltpu.make_async_copy(
                    bsend.at[it, r], piece_slot(it, r, xl), piece_recv.at[it, r, xl]).start()

            @pl.when(jnp.logical_not(own_k))
            def _():
                piece_near(it, r).start()

        def pieces_wait(it, r):
            for lo in range(2):
                pltpu.make_async_copy(
                    bsend.at[it, r], piece_slot(it, r, lo), piece_recv.at[it, r, lo]).wait()

        def product_of(it, r, distance):
            k = ((y if it == 0 else z) + distance) % RING
            return lax.dot_general(bbuf[it, r, k], gbuf[r, k], ROWS_T, preferred_element_type=F32)

        def first_products(it, r, start_at, count):
            acc[it, r] = jnp.zeros((128, 256), F32)

            @pl.loop(0, count)
            def _(j):
                acc[it, r] += product_of(it, r, start_at + j)

        def add_products(it, r, distances):
            total = acc[it, r]
            for distance in distances:
                total = total + product_of(it, r, distance)
            acc[it, r] = total

        def part_copy(it, r):
            return remote(acc.at[it, r, own_half(1 - xl)], precv.at[it, r],
                          part_send.at[it, r], part_recv.at[it, r], device(1, lo=1 - xl))

        def step_of(r):
            return step_size[r], step_size[r] * penalty[r]

        def next_beta(it, r, beta):
            step, threshold = step_of(r)
            part_copy(it, r).wait_recv()
            product = acc[it, r, own_half(xl)] + precv[it, r]
            return soften(beta - step * (product - cross_fit[r]), threshold)

        for copy in loads:
            copy.wait()
        gbuf[1, y] = gram_state[0].astype(BF16)
        cross_fit[1] = cross_state[0]
        step, threshold = step_of(1)
        beta_one = soften(step * cross_state[0], threshold)
        bsend[0, 1] = beta_one.astype(BF16)
        pl.semaphore_wait(barrier, len(peers))

        ring_start(GRAM, 1)
        pieces_start(0, 1)
        cross_feed = remote(cross_state.at[0], cross_fit.at[0], feed_send.at[1], feed_recv.at[1], device(0))
        gram_feed = remote(gsend, gbuf.at[0, y], feed_send.at[0], feed_recv.at[0], device(0))
        @pl.loop(1, 4)
        def _(hop):
            for r in (1, 0):
                ring_step(GRAM, r, hop)

            @pl.when(hop == 1)
            def _():
                for r in (1, 0):
                    pieces_wait(0, r)
                    ring_start(BETA, r)

            for r in (1, 0):
                ring_step(BETA, r, hop)

        for r in (1, 0):
            ring_last(BETA, r)
        cross_feed.wait_recv()
        step, threshold = step_of(0)
        beta_zero = soften(step * cross_fit[0], threshold)
        gram_feed.wait_recv()
        for r in (1, 0):
            first_products(0, r, 5, 7)
        for r in (1, 0):
            ring_last(GRAM, r)
            add_products(0, r, (4,))
            start(part_copy(0, r))
        betas = [beta_zero, beta_one]
        for r in (1, 0):
            betas[r] = next_beta(0, r, betas[r])
            bsend[1, r] = betas[r].astype(BF16)
            pieces_start(1, r)
        beta_keep[...] = betas[0]
        start(remote(beta_keep, end_beta, end_send.at[2], end_recv.at[2], device(0)))
        def reach_copy(r, slot, chunk, to):
            view = bbuf.at[1, r, chunk % RING]
            return remote(view, view, reach_send.at[r, slot], reach_recv.at[r, slot],
                          device(1, zz=(z + to) % RING))

        M1, P1, M2, P2, M3, P3, FAR = range(7)
        for r in (1, 0):
            pieces_wait(1, r)
            start(reach_copy(r, M2, z, 2))
            start(reach_copy(r, P2, z, 6))
            start(reach_copy(r, M1, z, 1))
            start(reach_copy(r, P1, z, 7))
        for r in (1, 0):
            reach_copy(r, M2, z + 6, 2).wait_recv()
            start(reach_copy(r, M3, z + 6, 1))
            if r == 0:
                start(reach_copy(r, FAR, z + 6, 2))
            reach_copy(r, P2, z + 2, 6).wait_recv()
            start(reach_copy(r, P3, z + 2, 7))
            if r == 1:
                start(reach_copy(r, FAR, z + 2, 6))
        for r in (1, 0):
            reach_copy(r, M1, z + 7, 1).wait_recv()
            reach_copy(r, P1, z + 1, 7).wait_recv()
            first_products(1, r, 6, 5)

        def last_products(r):
            reach_copy(r, M3, z + 5, 1).wait_recv()
            reach_copy(r, P3, z + 3, 7).wait_recv()
            reach_copy(r, FAR, z + 4, 2).wait_recv()
            add_products(1, r, (3, 4, 5))

        last_products(1)
        start(part_copy(1, 1))
        last_products(0)
        start(remote(acc.at[1, 0, own_half(1 - xl)], end_part.at[1], end_send.at[1], end_recv.at[1],
                     device(0, lo=1 - xl)))
        start(remote(acc.at[1, 0, own_half(xl)], end_part.at[0], end_send.at[0], end_recv.at[0], device(0)))
        remote(own_block.at[1], own_block.at[0], own_send, own_recv, device(0)).wait_recv()
        finish_sums()
        coef_out[...] = next_beta(1, 1, betas[1])

        for copy in sent:
            copy.wait_send()
        ring_drain(GRAM, 1)
        ring_drain(GRAM, 0, 2)
        for r in range(2):
            ring_drain(BETA, r)
        for it, r in ((0, 1), (1, 0), (1, 1)):
            @pl.when(jnp.logical_not(own_k))
            def _():
                piece_near(it, r).wait_send()

    @pl.when(c == 0)
    def _():
        COLS, ROWS, TARGETS = 0, 1, 2
        row0 = pl.multiple_of(xl * 192, 16)
        row0_other = pl.multiple_of((1 - xl) * 192, 16)
        part_h, part_q = y // 4, y % 4
        rows_h = pl.multiple_of(xl * 192 + part_h * 96, 16)

        def at96(index):
            return pl.ds(pl.multiple_of(index * 96, 16), 96)

        def expr_cols(index):
            return pl.ds(pl.multiple_of(index * 512 + part_q * 128, 128), 128)

        peers = [device(0, zz=(z + d) % RING) for d in range(1, RING)]
        peers += [device(core, yy=(y + d) % RING) for core in (0, 1) for d in (1, 7)]
        peers += [chip_x(right, 0), chip_x(left, 0), device(1)]
        peers += [chip_x((x + d) % 4, 1) for d in (1, 2, 3)]
        greet(peers)
        loads = [
            load(0, step_hbm, step_size), load(1, penalty_hbm, penalty), load(2, cross_hbm, cross_state),
            load(3, gram_hbm, gram_state),
        ]
        def stage_copy(d):
            return pltpu.make_async_copy(
                expr.at[pl.ds(rows_h, 96), expr_cols((z + d) % RING)], stage.at[d], stage_sem.at[d])

        def spread_copy(d, to, source):
            return remote(stage.at[d], rbuf.at[y, at96(source)], spread_send.at[d - 1], spread_recv.at[d - 1],
                          device(0, zz=to))

        @pl.loop(1, RING)
        def _(d):
            stage_copy(d).start()

        local = [
            pltpu.make_async_copy(
                expr.at[pl.ds(pl.multiple_of(row0 + h * 96, 16), 96), pl.ds(pl.multiple_of(y * 512, 512), 512)],
                cbuf.at[h, z], local_sem.at[h])
            for h in range(2)
        ]
        local.append(pltpu.make_async_copy(
            expr.at[pl.ds(rows_h, 96), expr_cols(z)], rbuf.at[y, at96(z)], local_sem.at[2]))
        for copy in local:
            copy.start()
        loads += [load(4, target_hbm, target), load(5, subsample_hbm, subsample)]
        sent = []

        def start(copy):
            copy.start()
            sent.append(copy)

        def view_of(ring, part, chunk):
            if ring == COLS:
                return cbuf.at[part, chunk]
            if ring == TARGETS:
                return tbuf.at[chunk]
            return rbuf.at[chunk, pl.ds(part * 384, 384)]

        ring_start, ring_step, ring_last, ring_drain = rings(0, view_of, (ROWS,))

        for copy in loads[:4]:
            copy.wait()
        gsend[...] = gram_state[0].astype(BF16)
        step = step_size[0]
        threshold = step * penalty[0]
        bsend_zero[...] = soften(step * cross_state[0], threshold).astype(BF16)
        pl.semaphore_wait(barrier, len(peers))

        for way in range(2):
            start(remote(gsend, gbuf.at[0, y], first_send.at[way], ring_recv.at[0, way, 0],
                         device(1, yy=(y + (7 if way else 1)) % RING)))
        for i, hi in enumerate((1 - xh, xh)):
            start(remote(bsend_zero, bbuf.at[0, 0, z, pl.ds(pl.multiple_of(xl * 64, 64), 64)], first_send.at[2 + i],
                         piece_recv.at[0, 0, xl], device(1, hi=hi, lo=xh)))
        @pl.loop(1, RING)
        def _(d):
            stage_copy(d).wait()
            spread_copy(d, (z + d) % RING, z).start()

        for copy in local:
            copy.wait()
        for part in range(2):
            ring_start(COLS, part)
        start(remote(gsend, gbuf.at[0, y], feed_send.at[0], feed_recv.at[0], device(1)))
        start(remote(cross_state.at[0], cross_fit.at[0], feed_send.at[1], feed_recv.at[1], device(1)))
        loads[4].wait()
        both = jnp.concatenate([target[...], target[...]], axis=0)
        lane_half = lax.broadcasted_iota(jnp.int32, both.shape, 0) // 64
        both = jnp.where(lane_half == xl, both, jnp.zeros_like(both))
        tpad[...] = both.T
        tsend[...] = tpad[pl.ds(row0_other, 192), :]
        swap = remote(tsend, trecv, swap_send, swap_recv, device(0, lo=1 - xl))
        start(swap)
        @pl.loop(1, RING)
        def _(d):
            spread_copy(d, z, (z + RING - d) % RING).wait_recv()

        for part in range(2):
            ring_start(ROWS, part)
        swap.wait_recv()
        for h in range(2):
            tbuf[z, h] = (
                tpad[pl.ds(pl.multiple_of(row0 + h * 96, 16), 96), :] + trecv[h * 96:(h + 1) * 96, :])
        ring_start(TARGETS, 0)

        loads[5].wait()
        first_lane = xh * 384 + xl * 192
        lane = lax.broadcasted_iota(jnp.int32, (2, 768), 1)
        for h in range(2):
            weights = jnp.zeros((2, 768), F32)
            for zz in range(RING):
                cells = subsample[:, zz * 768:(zz + 1) * 768].astype(F32)
                moved = pltpu.roll(cells, (1536 + zz * 96 - h * 96 - first_lane) % 768, axis=1)
                weights = jnp.where((lane >= zz * 96) & (lane < zz * 96 + 96), moved, weights)
            wbuf[h] = weights

        def weigh(distance):
            chunk = (y + distance) % RING
            h, q = chunk // 4, chunk % 4
            block = rbuf[chunk].T
            rows = pl.ds(pl.multiple_of(q * 128, 128), 128)
            pair = wbuf[h].astype(BF16)
            for r in range(2):
                lhs[r, h, rows, :] = block * pair[r:r + 1, :]

        @pl.loop(1, 4)
        def _(hop):
            for part in range(2):
                ring_step(ROWS, part, hop)
            for part in range(2):
                ring_step(COLS, part, hop)
            ring_step(TARGETS, 0, hop)

            @pl.loop(0, 2)
            def _(way):
                weigh((hop - 1) * (1 + 6 * way) % RING)

        for part in range(2):
            ring_last(COLS, part)
        ring_last(TARGETS, 0)

        @pl.loop(0, 2)
        def _(way):
            weigh(3 + 2 * way)

        for part in range(2):
            ring_last(ROWS, part)
        weigh(4)

        def rows_of(hi, h):
            half = pl.ds(pl.multiple_of(hi * 256, 256), 256)
            return jnp.concatenate([lhs[0, h, half, :], lhs[1, h, half, :]], axis=0)

        @pl.loop(0, 2)
        def _(hi):
            total = jnp.zeros((512, 128), F32)
            for h in range(2):
                total += jnp.dot(rows_of(hi, h), tbuf[:, h].reshape(768, 128), preferred_element_type=F32)
            for r in range(2):
                crosses[hi, r] = total[r * 256:(r + 1) * 256].T

        def crosses_of(r, index):
            return crosses[index // 2, r, pl.ds(pl.multiple_of((index % 2) * 64, 64), 64), :]

        top, low = pl.ds(0, 160), pl.ds(160, 160)

        def far_copy(r, half):
            rows = low if half else top
            return remote(xsend.at[r, 0, rows], xpass.at[r, rows], far_send.at[r, half], far_recv.at[r, half],
                          chip_x(left if half else right, 0))

        def near_copy(r, way, half):
            rows = low if half else top
            return remote(xsend.at[r, 1 + way, rows], xrecv.at[way, rows], near_send.at[r, way, half],
                          near_recv.at[way, half], chip_x(left if way else right, r))

        far = (x + 2) % 4

        @pl.loop(0, 4)
        def _(k):
            index = (x + 2 + 3 * k + 3 * (k // 2) + 2 * (k // 3)) % 4
            hi, lo = index // 2, index % 2
            total = jnp.zeros((512, 256), F32)
            for h in range(2):
                cols = cbuf[h, :, :, pl.ds(pl.multiple_of(lo * 256, 256), 256)].reshape(768, 256)
                total += jnp.dot(rows_of(hi, h), cols, preferred_element_type=F32)
            blocks[k] = total

            @pl.when(k == 0)
            def _():
                for r in (1, 0):
                    xsend[r, 0, 0:256, :] = blocks[0, r * 256:(r + 1) * 256].astype(BF16)
                    xsend[r, 0, 256:320, :] = crosses_of(r, far).astype(BF16)
                    far_copy(r, 0).start()
                    far_copy(r, 1).start()

            @pl.when(k == 1)
            def _():
                for r in (1, 0):
                    xsend[r, 1, 160:256, :] = blocks[1, r * 256 + 160:(r + 1) * 256].astype(BF16)
                    xsend[r, 1, 256:320, :] = crosses_of(r, right).astype(BF16)
                    near_copy(r, 0, 1).start()

            @pl.when(k == 2)
            def _():
                for r in (1, 0):
                    xsend[r, 2, 0:160, :] = blocks[2, r * 256:r * 256 + 160].astype(BF16)
                    near_copy(r, 1, 0).start()

        for r in (1, 0):
            far_copy(r, 0).wait_recv()
            xsend[r, 1, 0:160, :] = (
                blocks[1, r * 256:r * 256 + 160] + xpass[r, 0:160, :].astype(F32)).astype(BF16)
            near_copy(r, 0, 0).start()
            far_copy(r, 1).wait_recv()
            xsend[r, 2, 160:256, :] = (
                blocks[2, r * 256 + 160:(r + 1) * 256] + xpass[r, 160:256, :].astype(F32)).astype(BF16)
            xsend[r, 2, 256:320, :] = (crosses_of(r, left) + xpass[r, 256:320, :].astype(F32)).astype(BF16)
            near_copy(r, 1, 1).start()
        for r in (1, 0):
            own_block[r, 0:256, :] = blocks[3, r * 256:(r + 1) * 256]
            own_block[r, 256:320, :] = crosses_of(r, x)
        start(remote(own_block.at[1], own_block.at[0], own_send, own_recv, device(1)))

        finish_sums()
        for i in range(3):
            remote(end_beta, end_beta if i == 2 else end_part.at[i], end_send.at[i], end_recv.at[i],
                   device(1)).wait_recv()
        product = end_part[0] + end_part[1]
        coef_out[...] = soften(end_beta[...] - step * (product - cross_state[0]), threshold)
        for copy in sent:
            copy.wait_send()
        for part in range(2):
            ring_drain(COLS, part)
            ring_drain(ROWS, part)
        ring_drain(TARGETS, 0)

        @pl.loop(1, RING)
        def _(d):
            spread_copy(d, (z + d) % RING, z).wait_send()

        for r in range(2):
            for half in range(2):
                far_copy(r, half).wait_send()
                for way in range(2):
                    near_copy(r, way, half).wait_send()


def copy_out(gram, cross, coef, gram_out, cross_out, coef_out, gram_here, cross_here, coef_here, sems_in, sems_out):
    stages = ((gram, gram_here, gram_out), (cross, cross_here, cross_out), (coef, coef_here, coef_out))
    ins = [pltpu.make_async_copy(source, here, sems_in.at[i]) for i, (source, here, _) in enumerate(stages)]
    outs = [pltpu.make_async_copy(here, out, sems_out.at[i]) for i, (_, here, out) in enumerate(stages)]
    for copy in ins:
        copy.start()
    for arrived, copy in zip(ins, outs):
        arrived.wait()
        copy.start()
    for copy in outs:
        copy.wait()


def body(expr_stretch, target_stretch, subsample, gram_state, cross_state, step_size, penalty):
    vmem = pl.BlockSpec(memory_space=pltpu.VMEM)
    hbm = pl.BlockSpec(memory_space=pltpu.HBM)
    dma = pltpu.SemaphoreType.DMA
    out_shape = (
        jax.ShapeDtypeStruct((256, 256), F32),
        jax.ShapeDtypeStruct((64, 256), F32),
        jax.ShapeDtypeStruct((64, 256), F32),
    )
    results = pl.pallas_call(
        kernel,
        out_shape=out_shape,
        in_specs=[hbm] * 7,
        out_specs=(vmem, vmem, vmem),
        scratch_shapes=[
            pltpu.VMEM((64, 384), BF16),
            pltpu.VMEM((2, CELLS), jnp.int32),
            pltpu.VMEM((2, 256, 256), F32),
            pltpu.VMEM((2, 64, 256), F32),
            pltpu.SMEM((2,), F32),
            pltpu.SMEM((2,), F32),
            pltpu.VMEM((2, RING, 256, 256), BF16),
            pltpu.VMEM((2, 2, RING, 128, 256), BF16),
            pltpu.VMEM((2, 64, 256), F32),
            pltpu.VMEM((2, 2, 64, 256), BF16),
            pltpu.VMEM((2, 2, 128, 256), F32),
            pltpu.VMEM((2, 2, 64, 256), F32),
            pltpu.VMEM((64, 256), BF16),
            pltpu.VMEM((RING, 96, 128), BF16),
            pltpu.VMEM((2, RING, 96, 512), BF16),
            pltpu.VMEM((RING, 2, 96, 128), BF16),
            pltpu.VMEM((RING, 768, 128), BF16),
            pltpu.VMEM((2, 2, 512, 768), BF16),
            pltpu.VMEM((384, 128), BF16),
            pltpu.VMEM((192, 128), BF16),
            pltpu.VMEM((192, 128), BF16),
            pltpu.VMEM((2, 2, 128, 256), F32),
            pltpu.VMEM((2, 2, 768), F32),
            pltpu.VMEM((256, 256), BF16),
            pltpu.VMEM((4, 512, 256), F32),
            pltpu.VMEM((2, 3, 320, 256), BF16),
            pltpu.VMEM((2, 320, 256), BF16),
            pltpu.VMEM((2, 320, 256), F32),
            pltpu.VMEM((2, 320, 256), BF16),
            pltpu.VMEM((2, 64, 256), F32),
            pltpu.VMEM((64, 256), F32),
            pltpu.VMEM((64, 256), F32),
            dma((6, 2, 4)), dma((6, 2, 4)),
            dma((7,)), dma((7,)),
            dma((2, 2, 2)), dma((2, 2, 2)),
            dma((2, 2)), dma((2, 2)),
            dma((2, 2)), dma((2, 2)),
            dma((2, 2, 2)), dma((2, 2)),
            dma((2,)), dma((2,)),
            dma((3,)), dma((3,)),
            dma, dma,
            dma, dma,
            dma((3,)),
            dma((6,)),
            dma((RING,)),
            dma((4,)),
            dma((2, 7)), dma((2, 7)),
        ],
        compiler_params=pltpu.CompilerParams(
            collective_id=0, has_side_effects=True, vmem_limit_bytes=60 * 2**20),
    )(
        expr_stretch,
        target_stretch.T,
        subsample,
        gram_state[:, 0],
        jnp.swapaxes(cross_state[:, 0], 1, 2),
        step_size,
        penalty,
    )
    gram, cross, coef = pl.pallas_call(
        copy_out,
        out_shape=out_shape,
        in_specs=[hbm] * 3,
        out_specs=(hbm, hbm, hbm),
        scratch_shapes=[
            pltpu.VMEM((256, 256), F32),
            pltpu.VMEM((64, 256), F32),
            pltpu.VMEM((64, 256), F32),
            dma((3,)),
            dma((3,)),
        ],
        compiler_params=pltpu.CompilerParams(vmem_limit_bytes=60 * 2**20),
    )(*results)
    return gram[None], cross.T[None], coef.T[None]


def solution(mesh):
    return jax.shard_map(
        body,
        mesh=mesh,
        in_specs=(
            P("reg", None),
            P("reg", "tgt"),
            P(),
            P(None, "grp", "reg", "tgt"),
            P(None, "grp", "reg", "tgt"),
            P(),
            P(),
        ),
        out_specs=(P("grp", "reg", "tgt"), P("grp", "reg", "tgt"), P("grp", "reg", "tgt")),
        check_vma=False,
    )
```

```python
import jax
import jax.numpy as jnp
from jax import lax
from jax.experimental import pallas as pl
from jax.experimental.pallas import tpu as pltpu
from jax.sharding import PartitionSpec as P

RING = 8
CELLS = 6144
F32, BF16 = jnp.float32, jnp.bfloat16
ROWS_T = (((1,), (1,)), ((), ()))


def soften(values, threshold):
    return values - jnp.clip(values, -threshold, threshold)


def kernel(
    expr, target_hbm, subsample_hbm, gram_hbm, cross_hbm, step_hbm, penalty_hbm,
    gram_out, cross_out, coef_out,
    target, subsample, gram_state, cross_state, step_size, penalty,
    gbuf, bbuf, cross_fit, bsend, acc, precv,
    bsend_zero, stage, cbuf, tbuf, rbuf, lhs, tpad, tsend, trecv, crosses, wbuf, gsend,
    blocks, xsend, xpass, own_block, xrecv, end_part, end_beta, beta_keep,
    ring_send, ring_recv, spread_send, spread_recv, piece_send, piece_recv,
    part_send, part_recv, far_send, far_recv, near_send, near_recv,
    feed_send, feed_recv, end_send, end_recv, own_send, own_recv,
    swap_send, swap_recv, local_sem, load_sem, stage_sem, first_send, reach_send, reach_recv,
):
    c = lax.axis_index("grp")
    reg = lax.axis_index("reg")
    tgt = lax.axis_index("tgt")
    z, xh = reg // 2, reg % 2
    y, xl = tgt // 2, tgt % 2
    x = xh * 2 + xl

    def device(core, zz=z, hi=xh, yy=y, lo=xl):
        return (core, zz * 2 + hi, yy * 2 + lo)

    def chip_x(index, core):
        return device(core, hi=index // 2, lo=index % 2)

    def remote(src, dst, send, recv, to):
        return pltpu.make_async_remote_copy(
            src_ref=src, dst_ref=dst, send_sem=send, recv_sem=recv,
            device_id=to, device_id_type=pl.DeviceIdType.MESH,
        )

    right, left = (x + 1) % 4, (x + 3) % 4
    barrier = pltpu.get_barrier_semaphore()

    def greet(peers):
        for peer in peers:
            pl.semaphore_signal(barrier, inc=1, device_id=peer, device_id_type=pl.DeviceIdType.MESH)

    def load(index, source, here):
        copy = pltpu.make_async_copy(source, here, load_sem.at[index])
        copy.start()
        return copy

    def rings(core, view_of, along_y):
        def ring_copy(ring, part, way, hop, chunk):
            here = y if ring in along_y else z
            there = (here + (1 if way == 0 else RING - 1)) % RING
            view = view_of(ring, part, chunk)
            slot = ring * 2 + part
            return remote(view, view, ring_send.at[slot, way, hop - 1], ring_recv.at[slot, way, hop - 1],
                          device(core, yy=there) if ring in along_y else device(core, zz=there))

        def ring_start(ring, part):
            here = y if ring in along_y else z
            for way in range(2):
                ring_copy(ring, part, way, 1, here).start()

        def arrived(ring, way, hop):
            here = y if ring in along_y else z
            return (here + (RING - hop if way == 0 else hop)) % RING

        def ring_step(ring, part, hop):
            for way in range(2):
                chunk = arrived(ring, way, hop)
                ring_copy(ring, part, way, hop, chunk).wait_recv()
                if way == part:
                    ring_copy(ring, part, way, hop + 1, chunk).start()
                else:
                    @pl.when(hop < 3)
                    def _():
                        ring_copy(ring, part, way, hop + 1, chunk).start()

        def ring_last(ring, part):
            ring_copy(ring, part, part, 4, arrived(ring, part, 4)).wait_recv()

        def ring_drain(ring, part, first=1):
            @pl.loop(first, 5)
            def _(hop):
                for way in range(2):
                    copy = ring_copy(ring, part, way, hop, arrived(ring, way, hop - 1))
                    if way == part:
                        copy.wait_send()
                    else:
                        pl.when(hop < 4)(copy.wait_send)

        return ring_start, ring_step, ring_last, ring_drain

    def finish_sums():
        for way in range(2):
            for half in range(2):
                rows = pl.ds(160 * half, 160)
                remote(xsend.at[0, 1 + way, rows], xrecv.at[way, rows], near_send.at[0, way, half],
                       near_recv.at[way, half], chip_x(left if way else right, 0)).wait_recv()
        sums = own_block[0] + xrecv[0].astype(F32) + xrecv[1].astype(F32)
        gram_out[...] = gram_state[1] + sums[0:256] / CELLS
        cross_out[...] = cross_state[1] + sums[256:320] / CELLS

    @pl.when(c == 1)
    def _():
        GRAM, BETA = 0, 1
        loads = [
            load(0, step_hbm, step_size), load(1, penalty_hbm, penalty),
            load(2, cross_hbm, cross_state), load(3, gram_hbm, gram_state),
        ]
        peers = [device(1, zz=(z + d) % RING) for d in (1, 2, 6, 7)]
        peers += [device(core, yy=(y + d) % RING) for core in (0, 1) for d in (1, 7)]
        peers += [chip_x((x + d) % 4, core) for core in (0, 1) for d in (1, 2, 3)]
        peers += [device(0)]
        greet(peers)
        sent = []

        def start(copy):
            copy.start()
            sent.append(copy)

        def view_of(ring, part, chunk):
            if ring == GRAM:
                return gbuf.at[part, chunk]
            return bbuf.at[ring - BETA, part, chunk]

        ring_start, ring_step, ring_last, ring_drain = rings(1, view_of, (GRAM,))
        own_k = xl == xh

        def own_half(ref_index):
            return pl.ds(pl.multiple_of(ref_index * 64, 64), 64)

        def piece_slot(it, r, lo):
            return bbuf.at[it, r, z, own_half(lo)]

        def piece_near(it, r):
            return remote(bsend.at[it, r], piece_slot(it, r, xl), piece_send.at[it, r, 1],
                          piece_recv.at[it, r, xl], device(1, lo=1 - xl))

        def pieces_start(it, r):
            start(remote(bsend.at[it, r], piece_slot(it, r, xl), piece_send.at[it, r, 0],
                         piece_recv.at[it, r, xl], device(1, hi=1 - xh, lo=xh)))

            @pl.when(own_k)
            def _():
                pltpu.make_async_copy(
                    bsend.at[it, r], piece_slot(it, r, xl), piece_recv.at[it, r, xl]).start()

            @pl.when(jnp.logical_not(own_k))
            def _():
                piece_near(it, r).start()

        def pieces_wait(it, r):
            for lo in range(2):
                pltpu.make_async_copy(
                    bsend.at[it, r], piece_slot(it, r, lo), piece_recv.at[it, r, lo]).wait()

        def product_of(it, r, distance):
            k = ((y if it == 0 else z) + distance) % RING
            return lax.dot_general(bbuf[it, r, k], gbuf[r, k], ROWS_T, preferred_element_type=F32)

        def first_products(it, r, start_at, count):
            acc[it, r] = jnp.zeros((128, 256), F32)

            @pl.loop(0, count)
            def _(j):
                acc[it, r] += product_of(it, r, start_at + j)

        def add_products(it, r, distances):
            total = acc[it, r]
            for distance in distances:
                total = total + product_of(it, r, distance)
            acc[it, r] = total

        def part_copy(it, r):
            return remote(acc.at[it, r, own_half(1 - xl)], precv.at[it, r],
                          part_send.at[it, r], part_recv.at[it, r], device(1, lo=1 - xl))

        def step_of(r):
            return step_size[r], step_size[r] * penalty[r]

        def next_beta(it, r, beta):
            step, threshold = step_of(r)
            part_copy(it, r).wait_recv()
            product = acc[it, r, own_half(xl)] + precv[it, r]
            return soften(beta - step * (product - cross_fit[r]), threshold)

        for copy in loads:
            copy.wait()
        gbuf[1, y] = gram_state[0].astype(BF16)
        cross_fit[1] = cross_state[0]
        step, threshold = step_of(1)
        beta_one = soften(step * cross_state[0], threshold)
        bsend[0, 1] = beta_one.astype(BF16)
        pl.semaphore_wait(barrier, len(peers))

        ring_start(GRAM, 1)
        pieces_start(0, 1)
        cross_feed = remote(cross_state.at[0], cross_fit.at[0], feed_send.at[1], feed_recv.at[1], device(0))
        gram_feed = remote(gsend, gbuf.at[0, y], feed_send.at[0], feed_recv.at[0], device(0))
        for r in (1, 0):
            pieces_wait(0, r)
            ring_start(BETA, r)

        @pl.loop(1, 4)
        def _(hop):
            for r in (1, 0):
                ring_step(GRAM, r, hop)
            for r in (1, 0):
                ring_step(BETA, r, hop)

        for r in (1, 0):
            ring_last(BETA, r)
        cross_feed.wait_recv()
        step, threshold = step_of(0)
        beta_zero = soften(step * cross_fit[0], threshold)
        gram_feed.wait_recv()
        for r in (1, 0):
            first_products(0, r, 5, 7)
        for r in (1, 0):
            ring_last(GRAM, r)
            add_products(0, r, (4,))
            start(part_copy(0, r))
        betas = [beta_zero, beta_one]
        for r in (1, 0):
            betas[r] = next_beta(0, r, betas[r])
            bsend[1, r] = betas[r].astype(BF16)
            pieces_start(1, r)
        beta_keep[...] = betas[0]
        start(remote(beta_keep, end_beta, end_send.at[2], end_recv.at[2], device(0)))
        def reach_copy(r, slot, chunk, to):
            view = bbuf.at[1, r, chunk % RING]
            return remote(view, view, reach_send.at[r, slot], reach_recv.at[r, slot],
                          device(1, zz=(z + to) % RING))

        M1, P1, M2, P2, M3, P3, FAR = range(7)
        for r in (1, 0):
            pieces_wait(1, r)
            start(reach_copy(r, M2, z, 2))
            start(reach_copy(r, P2, z, 6))
            start(reach_copy(r, M1, z, 1))
            start(reach_copy(r, P1, z, 7))
        for r in (1, 0):
            reach_copy(r, M2, z + 6, 2).wait_recv()
            start(reach_copy(r, M3, z + 6, 1))
            if r == 0:
                start(reach_copy(r, FAR, z + 6, 2))
            reach_copy(r, P2, z + 2, 6).wait_recv()
            start(reach_copy(r, P3, z + 2, 7))
            if r == 1:
                start(reach_copy(r, FAR, z + 2, 6))
        for r in (1, 0):
            reach_copy(r, M1, z + 7, 1).wait_recv()
            reach_copy(r, P1, z + 1, 7).wait_recv()
            first_products(1, r, 6, 5)

        def last_products(r):
            reach_copy(r, M3, z + 5, 1).wait_recv()
            reach_copy(r, P3, z + 3, 7).wait_recv()
            reach_copy(r, FAR, z + 4, 2).wait_recv()
            add_products(1, r, (3, 4, 5))

        last_products(1)
        start(part_copy(1, 1))
        last_products(0)
        start(remote(acc.at[1, 0, own_half(1 - xl)], end_part.at[1], end_send.at[1], end_recv.at[1],
                     device(0, lo=1 - xl)))
        start(remote(acc.at[1, 0, own_half(xl)], end_part.at[0], end_send.at[0], end_recv.at[0], device(0)))
        remote(own_block.at[1], own_block.at[0], own_send, own_recv, device(0)).wait_recv()
        finish_sums()
        coef_out[...] = next_beta(1, 1, betas[1])

        for copy in sent:
            copy.wait_send()
        ring_drain(GRAM, 1)
        ring_drain(GRAM, 0, 2)
        for r in range(2):
            ring_drain(BETA, r)
        for it, r in ((0, 1), (1, 0), (1, 1)):
            @pl.when(jnp.logical_not(own_k))
            def _():
                piece_near(it, r).wait_send()

    @pl.when(c == 0)
    def _():
        COLS, ROWS, TARGETS = 0, 1, 2
        row0 = pl.multiple_of(xl * 192, 16)
        row0_other = pl.multiple_of((1 - xl) * 192, 16)
        part_h, part_q = y // 4, y % 4
        rows_h = pl.multiple_of(xl * 192 + part_h * 96, 16)

        def at96(index):
            return pl.ds(pl.multiple_of(index * 96, 16), 96)

        def expr_cols(index):
            return pl.ds(pl.multiple_of(index * 512 + part_q * 128, 128), 128)

        peers = [device(0, zz=(z + d) % RING) for d in range(1, RING)]
        peers += [device(core, yy=(y + d) % RING) for core in (0, 1) for d in (1, 7)]
        peers += [chip_x(right, 0), chip_x(left, 0), device(1)]
        peers += [chip_x((x + d) % 4, 1) for d in (1, 2, 3)]
        greet(peers)
        loads = [
            load(0, step_hbm, step_size), load(1, penalty_hbm, penalty), load(2, cross_hbm, cross_state),
            load(3, gram_hbm, gram_state),
        ]
        def stage_copy(d):
            return pltpu.make_async_copy(
                expr.at[pl.ds(rows_h, 96), expr_cols((z + d) % RING)], stage.at[d], stage_sem.at[d])

        def spread_copy(d, to, source):
            return remote(stage.at[d], rbuf.at[y, at96(source)], spread_send.at[d - 1], spread_recv.at[d - 1],
                          device(0, zz=to))

        @pl.loop(1, RING)
        def _(d):
            stage_copy(d).start()

        local = [
            pltpu.make_async_copy(
                expr.at[pl.ds(pl.multiple_of(row0 + h * 96, 16), 96), pl.ds(pl.multiple_of(y * 512, 512), 512)],
                cbuf.at[h, z], local_sem.at[h])
            for h in range(2)
        ]
        local.append(pltpu.make_async_copy(
            expr.at[pl.ds(rows_h, 96), expr_cols(z)], rbuf.at[y, at96(z)], local_sem.at[2]))
        for copy in local:
            copy.start()
        loads += [load(4, target_hbm, target), load(5, subsample_hbm, subsample)]
        sent = []

        def start(copy):
            copy.start()
            sent.append(copy)

        def view_of(ring, part, chunk):
            if ring == COLS:
                return cbuf.at[part, chunk]
            if ring == TARGETS:
                return tbuf.at[chunk]
            return rbuf.at[chunk, pl.ds(part * 384, 384)]

        ring_start, ring_step, ring_last, ring_drain = rings(0, view_of, (ROWS,))

        for copy in loads[:4]:
            copy.wait()
        gsend[...] = gram_state[0].astype(BF16)
        step = step_size[0]
        threshold = step * penalty[0]
        bsend_zero[...] = soften(step * cross_state[0], threshold).astype(BF16)
        pl.semaphore_wait(barrier, len(peers))

        @pl.loop(1, RING)
        def _(d):
            stage_copy(d).wait()
            spread_copy(d, (z + d) % RING, z).start()

        for copy in local:
            copy.wait()
        for part in range(2):
            ring_start(COLS, part)
        for way in range(2):
            start(remote(gsend, gbuf.at[0, y], first_send.at[way], ring_recv.at[0, way, 0],
                         device(1, yy=(y + (7 if way else 1)) % RING)))
        for i, hi in enumerate((1 - xh, xh)):
            start(remote(bsend_zero, bbuf.at[0, 0, z, pl.ds(pl.multiple_of(xl * 64, 64), 64)], first_send.at[2 + i],
                         piece_recv.at[0, 0, xl], device(1, hi=hi, lo=xh)))
        start(remote(gsend, gbuf.at[0, y], feed_send.at[0], feed_recv.at[0], device(1)))
        start(remote(cross_state.at[0], cross_fit.at[0], feed_send.at[1], feed_recv.at[1], device(1)))
        loads[4].wait()
        both = jnp.concatenate([target[...], target[...]], axis=0)
        lane_half = lax.broadcasted_iota(jnp.int32, both.shape, 0) // 64
        both = jnp.where(lane_half == xl, both, jnp.zeros_like(both))
        tpad[...] = both.T
        tsend[...] = tpad[pl.ds(row0_other, 192), :]
        swap = remote(tsend, trecv, swap_send, swap_recv, device(0, lo=1 - xl))
        start(swap)
        @pl.loop(1, RING)
        def _(d):
            spread_copy(d, z, (z + RING - d) % RING).wait_recv()

        for part in range(2):
            ring_start(ROWS, part)
        swap.wait_recv()
        for h in range(2):
            tbuf[z, h] = (
                tpad[pl.ds(pl.multiple_of(row0 + h * 96, 16), 96), :] + trecv[h * 96:(h + 1) * 96, :])
        ring_start(TARGETS, 0)

        loads[5].wait()
        first_lane = xh * 384 + xl * 192
        lane = lax.broadcasted_iota(jnp.int32, (2, 768), 1)
        for h in range(2):
            weights = jnp.zeros((2, 768), F32)
            for zz in range(RING):
                cells = subsample[:, zz * 768:(zz + 1) * 768].astype(F32)
                moved = pltpu.roll(cells, (1536 + zz * 96 - h * 96 - first_lane) % 768, axis=1)
                weights = jnp.where((lane >= zz * 96) & (lane < zz * 96 + 96), moved, weights)
            wbuf[h] = weights

        def weigh(distance):
            chunk = (y + distance) % RING
            h, q = chunk // 4, chunk % 4
            block = rbuf[chunk].T
            rows = pl.ds(pl.multiple_of(q * 128, 128), 128)
            pair = wbuf[h].astype(BF16)
            for r in range(2):
                lhs[r, h, rows, :] = block * pair[r:r + 1, :]

        @pl.loop(1, 4)
        def _(hop):
            for part in range(2):
                ring_step(ROWS, part, hop)
            for part in range(2):
                ring_step(COLS, part, hop)
            ring_step(TARGETS, 0, hop)

            @pl.loop(0, 2)
            def _(way):
                weigh((hop - 1) * (1 + 6 * way) % RING)

        for part in range(2):
            ring_last(COLS, part)
        ring_last(TARGETS, 0)

        @pl.loop(0, 2)
        def _(way):
            weigh(3 + 2 * way)

        for part in range(2):
            ring_last(ROWS, part)
        weigh(4)

        def rows_of(hi, h):
            half = pl.ds(pl.multiple_of(hi * 256, 256), 256)
            return jnp.concatenate([lhs[0, h, half, :], lhs[1, h, half, :]], axis=0)

        @pl.loop(0, 2)
        def _(hi):
            total = jnp.zeros((512, 128), F32)
            for h in range(2):
                total += jnp.dot(rows_of(hi, h), tbuf[:, h].reshape(768, 128), preferred_element_type=F32)
            for r in range(2):
                crosses[hi, r] = total[r * 256:(r + 1) * 256].T

        def crosses_of(r, index):
            return crosses[index // 2, r, pl.ds(pl.multiple_of((index % 2) * 64, 64), 64), :]

        top, low = pl.ds(0, 160), pl.ds(160, 160)

        def far_copy(r, half):
            rows = low if half else top
            return remote(xsend.at[r, 0, rows], xpass.at[r, rows], far_send.at[r, half], far_recv.at[r, half],
                          chip_x(left if half else right, 0))

        def near_copy(r, way, half):
            rows = low if half else top
            return remote(xsend.at[r, 1 + way, rows], xrecv.at[way, rows], near_send.at[r, way, half],
                          near_recv.at[way, half], chip_x(left if way else right, r))

        far = (x + 2) % 4

        @pl.loop(0, 4)
        def _(k):
            index = (x + 2 + 3 * k + 3 * (k // 2) + 2 * (k // 3)) % 4
            hi, lo = index // 2, index % 2
            total = jnp.zeros((512, 256), F32)
            for h in range(2):
                cols = cbuf[h, :, :, pl.ds(pl.multiple_of(lo * 256, 256), 256)].reshape(768, 256)
                total += jnp.dot(rows_of(hi, h), cols, preferred_element_type=F32)
            blocks[k] = total

            @pl.when(k == 0)
            def _():
                for r in (1, 0):
                    xsend[r, 0, 0:256, :] = blocks[0, r * 256:(r + 1) * 256].astype(BF16)
                    xsend[r, 0, 256:320, :] = crosses_of(r, far).astype(BF16)
                    far_copy(r, 0).start()
                    far_copy(r, 1).start()

            @pl.when(k == 1)
            def _():
                for r in (1, 0):
                    xsend[r, 1, 160:256, :] = blocks[1, r * 256 + 160:(r + 1) * 256].astype(BF16)
                    xsend[r, 1, 256:320, :] = crosses_of(r, right).astype(BF16)
                    near_copy(r, 0, 1).start()

            @pl.when(k == 2)
            def _():
                for r in (1, 0):
                    xsend[r, 2, 0:160, :] = blocks[2, r * 256:r * 256 + 160].astype(BF16)
                    near_copy(r, 1, 0).start()

        for r in (1, 0):
            far_copy(r, 0).wait_recv()
            xsend[r, 1, 0:160, :] = (
                blocks[1, r * 256:r * 256 + 160] + xpass[r, 0:160, :].astype(F32)).astype(BF16)
            near_copy(r, 0, 0).start()
            far_copy(r, 1).wait_recv()
            xsend[r, 2, 160:256, :] = (
                blocks[2, r * 256 + 160:(r + 1) * 256] + xpass[r, 160:256, :].astype(F32)).astype(BF16)
            xsend[r, 2, 256:320, :] = (crosses_of(r, left) + xpass[r, 256:320, :].astype(F32)).astype(BF16)
            near_copy(r, 1, 1).start()
        for r in (1, 0):
            own_block[r, 0:256, :] = blocks[3, r * 256:(r + 1) * 256]
            own_block[r, 256:320, :] = crosses_of(r, x)
        start(remote(own_block.at[1], own_block.at[0], own_send, own_recv, device(1)))

        finish_sums()
        for i in range(3):
            remote(end_beta, end_beta if i == 2 else end_part.at[i], end_send.at[i], end_recv.at[i],
                   device(1)).wait_recv()
        product = end_part[0] + end_part[1]
        coef_out[...] = soften(end_beta[...] - step * (product - cross_state[0]), threshold)
        for copy in sent:
            copy.wait_send()
        for part in range(2):
            ring_drain(COLS, part)
            ring_drain(ROWS, part)
        ring_drain(TARGETS, 0)

        @pl.loop(1, RING)
        def _(d):
            spread_copy(d, (z + d) % RING, z).wait_send()

        for r in range(2):
            for half in range(2):
                far_copy(r, half).wait_send()
                for way in range(2):
                    near_copy(r, way, half).wait_send()


def copy_out(gram, cross, coef, gram_out, cross_out, coef_out, gram_here, cross_here, coef_here, sems_in, sems_out):
    stages = ((gram, gram_here, gram_out), (cross, cross_here, cross_out), (coef, coef_here, coef_out))
    ins = [pltpu.make_async_copy(source, here, sems_in.at[i]) for i, (source, here, _) in enumerate(stages)]
    outs = [pltpu.make_async_copy(here, out, sems_out.at[i]) for i, (_, here, out) in enumerate(stages)]
    for copy in ins:
        copy.start()
    for arrived, copy in zip(ins, outs):
        arrived.wait()
        copy.start()
    for copy in outs:
        copy.wait()


def body(expr_stretch, target_stretch, subsample, gram_state, cross_state, step_size, penalty):
    vmem = pl.BlockSpec(memory_space=pltpu.VMEM)
    hbm = pl.BlockSpec(memory_space=pltpu.HBM)
    dma = pltpu.SemaphoreType.DMA
    out_shape = (
        jax.ShapeDtypeStruct((256, 256), F32),
        jax.ShapeDtypeStruct((64, 256), F32),
        jax.ShapeDtypeStruct((64, 256), F32),
    )
    results = pl.pallas_call(
        kernel,
        out_shape=out_shape,
        in_specs=[hbm] * 7,
        out_specs=(vmem, vmem, vmem),
        scratch_shapes=[
            pltpu.VMEM((64, 384), BF16),
            pltpu.VMEM((2, CELLS), jnp.int32),
            pltpu.VMEM((2, 256, 256), F32),
            pltpu.VMEM((2, 64, 256), F32),
            pltpu.SMEM((2,), F32),
            pltpu.SMEM((2,), F32),
            pltpu.VMEM((2, RING, 256, 256), BF16),
            pltpu.VMEM((2, 2, RING, 128, 256), BF16),
            pltpu.VMEM((2, 64, 256), F32),
            pltpu.VMEM((2, 2, 64, 256), BF16),
            pltpu.VMEM((2, 2, 128, 256), F32),
            pltpu.VMEM((2, 2, 64, 256), F32),
            pltpu.VMEM((64, 256), BF16),
            pltpu.VMEM((RING, 96, 128), BF16),
            pltpu.VMEM((2, RING, 96, 512), BF16),
            pltpu.VMEM((RING, 2, 96, 128), BF16),
            pltpu.VMEM((RING, 768, 128), BF16),
            pltpu.VMEM((2, 2, 512, 768), BF16),
            pltpu.VMEM((384, 128), BF16),
            pltpu.VMEM((192, 128), BF16),
            pltpu.VMEM((192, 128), BF16),
            pltpu.VMEM((2, 2, 128, 256), F32),
            pltpu.VMEM((2, 2, 768), F32),
            pltpu.VMEM((256, 256), BF16),
            pltpu.VMEM((4, 512, 256), F32),
            pltpu.VMEM((2, 3, 320, 256), BF16),
            pltpu.VMEM((2, 320, 256), BF16),
            pltpu.VMEM((2, 320, 256), F32),
            pltpu.VMEM((2, 320, 256), BF16),
            pltpu.VMEM((2, 64, 256), F32),
            pltpu.VMEM((64, 256), F32),
            pltpu.VMEM((64, 256), F32),
            dma((6, 2, 4)), dma((6, 2, 4)),
            dma((7,)), dma((7,)),
            dma((2, 2, 2)), dma((2, 2, 2)),
            dma((2, 2)), dma((2, 2)),
            dma((2, 2)), dma((2, 2)),
            dma((2, 2, 2)), dma((2, 2)),
            dma((2,)), dma((2,)),
            dma((3,)), dma((3,)),
            dma, dma,
            dma, dma,
            dma((3,)),
            dma((6,)),
            dma((RING,)),
            dma((4,)),
            dma((2, 7)), dma((2, 7)),
        ],
        compiler_params=pltpu.CompilerParams(
            collective_id=0, has_side_effects=True, vmem_limit_bytes=60 * 2**20),
    )(
        expr_stretch,
        target_stretch.T,
        subsample,
        gram_state[:, 0],
        jnp.swapaxes(cross_state[:, 0], 1, 2),
        step_size,
        penalty,
    )
    gram, cross, coef = pl.pallas_call(
        copy_out,
        out_shape=out_shape,
        in_specs=[hbm] * 3,
        out_specs=(hbm, hbm, hbm),
        scratch_shapes=[
            pltpu.VMEM((256, 256), F32),
            pltpu.VMEM((64, 256), F32),
            pltpu.VMEM((64, 256), F32),
            dma((3,)),
            dma((3,)),
        ],
        compiler_params=pltpu.CompilerParams(vmem_limit_bytes=60 * 2**20),
    )(*results)
    return gram[None], cross.T[None], coef.T[None]


def solution(mesh):
    return jax.shard_map(
        body,
        mesh=mesh,
        in_specs=(
            P("reg", None),
            P("reg", "tgt"),
            P(),
            P(None, "grp", "reg", "tgt"),
            P(None, "grp", "reg", "tgt"),
            P(),
            P(),
        ),
        out_specs=(P("grp", "reg", "tgt"), P("grp", "reg", "tgt"), P("grp", "reg", "tgt")),
        check_vma=False,
    )
```
